32 devices in a mesh: brick: 8 (over y, x, core), grp: 4 (over z).
Axes of the slice: x: 2, y: 2, z: 4, core: 2. Of those that a mesh axis runs over, the one named last changes fastest.
Arguments:
- features: bfloat16 [262144, 128], P(('brick', 'grp')), may hold values from -6 to 6
- neighbors: int32 [262144, 27], P(('brick', 'grp')), may hold values from 0 to 12288, as said below
- send_low: int32 [65536], P(('brick', 'grp')), may hold values from 0 to 8191, as said below
- send_high: int32 [65536], P(('brick', 'grp')), may hold values from 0 to 8191, as said below
- send_slot: int32 [393216], P(('brick', 'grp')), may hold values from 0 to 8192, as said below
- recv_slot: int32 [262144], P(('brick', 'grp')), may hold values from 0 to 12287, as said below
- kernel: bfloat16 [27, 128, 128], P(None, None, 'grp'), may hold values from -0.109375 to 0.109375
- norm_gain: float32 [128], replicated, may hold values from 0.5 to 1.5
- norm_shift: float32 [128], replicated, may hold values from -3 to 3
Outputs:
- serial: bfloat16 [262144, 128], P(('brick', 'grp'))
The draws below stay inside these ranges and needn't reach their ends.
Inputs may be any that keep to these rules, and one draw needn't show every extreme that they name: `neighbors`: an entry below 8192 is a row of the brick itself; 8192 + i is the i-th row sent up by the brick one slab lower; 10240 + i the i-th row sent down by the brick one slab higher; 12288 means no neighbour. Offset k = 9 (dx + 1) + 3 (dy + 1) + (dz + 1); offsets with dx = 0 refer only to the brick's own rows or to no neighbour; offset 13 is the voxel itself; no entry refers to a brick that does not exist. `send_low`: the 2048 entries of a brick are distinct rows of it. `send_high`: the 2048 entries of a brick are distinct rows of it. `send_slot`: 8192 marks an empty slot; every row of a brick is carried by exactly one slot; a brick fills between 512 and 1536 slots for each shard of its scan, the slots t * 1536 + c with c below that count, and every shard receives 8192 rows in all. `recv_slot`: the 8192 entries of a shard are exactly its filled received slots, each once.
All inputs are finite; a program needn't handle non-finite values.
Results may differ from the reference program's by a relative error of at most 0.001.
Values may be sent and summed in bfloat16 or wider, within the bound.
A program may use at most 64 MiB of HBM per device.

```python
import jax
import jax.numpy as jnp
from jax import lax

C = 128
KVOL = 27
V_DEV = 8192
HALO = 2048
BRICKS = 32
TOTAL = 262144
CAP = 1536
N_BRICK = 8
N_GRP = 4


def draw_neighbors(key, part):
    base = jax.random.fold_in(key, 11)
    shape = (TOTAL, KVOL)
    present = jax.random.randint(jax.random.fold_in(base, 1), shape, 0, 5) < 2
    local_pick = jax.random.randint(jax.random.fold_in(base, 2), shape, 0, V_DEV)
    halo_pick = jax.random.randint(jax.random.fold_in(base, 3), shape, 0, HALO)
    crossing = jax.random.randint(jax.random.fold_in(base, 4), shape, 0, 4) == 0
    offsets = jnp.arange(KVOL, dtype=jnp.int32)
    step_x = (offsets // 9 - 1)[None, :]
    row_ids = jnp.arange(TOTAL, dtype=jnp.int32)
    slab = row_ids // V_DEV // N_GRP
    below_ok = (slab > 0)[:, None]
    above_ok = (slab < N_BRICK - 1)[:, None]
    halo_index = jnp.where(step_x < 0, V_DEV + halo_pick, V_DEV + HALO + halo_pick)
    use_halo = crossing & (step_x != 0) & jnp.where(step_x < 0, below_ok, above_ok)
    chosen = jnp.where(use_halo, halo_index, local_pick)
    chosen = jnp.where(present, chosen, V_DEV + 2 * HALO)
    chosen = jnp.where(offsets[None, :] == 13, (row_ids % V_DEV)[:, None], chosen)
    return chosen.astype(jnp.int32)


def halo_rows(key, salt):
    keys = jax.random.split(jax.random.fold_in(key, salt), BRICKS)
    orders = jax.vmap(lambda single: jax.random.permutation(single, V_DEV))(keys)
    return orders[:, :HALO].reshape(-1).astype(jnp.int32)


def draw_send_low(key, part):
    return halo_rows(key, 21)


def draw_send_high(key, part):
    return halo_rows(key, 22)


def relay_tables(key):
    base = jax.random.fold_in(key, 7)
    swing = V_DEV // (2 * N_BRICK)
    share = 2 * swing
    capacity = share + swing
    parity = jax.random.randint(jax.random.fold_in(base, 1), (), 0, 2)
    positions = jnp.arange(V_DEV, dtype=jnp.int32)[None, :]
    devices = jnp.arange(BRICKS, dtype=jnp.int32)[:, None]
    slab_of = devices // N_GRP
    leading = 2 * (positions // (2 * share))
    within = positions % (2 * share)
    first_count = share + swing * (1 - 2 * ((slab_of + leading + parity) % 2))
    partner = jnp.where(within < first_count, leading, leading + 1)
    offset_in = jnp.where(within < first_count, within, within - first_count)
    slot_value = (partner * capacity + offset_in).astype(jnp.int32)
    send_keys = jax.random.split(jax.random.fold_in(base, 2), BRICKS)
    send_order = jax.vmap(lambda single: jax.random.permutation(single, V_DEV))(send_keys).astype(jnp.int32)
    send_table = jnp.full((BRICKS, N_BRICK * capacity), V_DEV, jnp.int32).at[devices, slot_value].set(send_order)
    recv_keys = jax.random.split(jax.random.fold_in(base, 3), BRICKS)
    recv_order = jax.vmap(lambda single: jax.random.permutation(single, V_DEV))(recv_keys).astype(jnp.int32)
    recv_table = jnp.take_along_axis(slot_value, recv_order, axis=1)
    return (send_table.reshape(-1).astype(jnp.int32), recv_table.reshape(-1).astype(jnp.int32))


def draw_send_slot(key, part):
    return relay_tables(key)[0]


def draw_recv_slot(key, part):
    return relay_tables(key)[1]


def shard_levels(stream_key, dims, pieces, least, top_value):
    loudness = 1.0
    for position, shards_of in pieces:
        heights = jax.random.uniform(jax.random.fold_in(jax.random.fold_in(stream_key, 6), position), (shards_of,), jnp.float32, least / len(pieces), top_value / len(pieces))
        loudness = loudness * jnp.repeat(jnp.exp(heights), dims[position] // shards_of).reshape((-1,) + (1,) * (len(dims) - 1 - position))
    return loudness


def gaussian(own_key, dims, width, reach, cuts=(), kind=jnp.bfloat16):
    loudness = shard_levels(own_key, dims, cuts, -0.22, 0.18) if cuts else 1.0
    result = jax.random.normal(own_key, dims, jnp.float32) * width * loudness
    return jnp.minimum(jnp.maximum(result, -reach), reach).astype(kind)


def setup_inputs(seed: int = 0) -> dict:
    key_of = jax.random.split(jax.random.key(seed), 10)
    return {
        "features": gaussian(key_of[0], (TOTAL, C), 1.0, 6.0, ((0, 32),)),
        "neighbors": draw_neighbors(jax.random.fold_in(key_of[9], 71), 0),
        "send_low": draw_send_low(jax.random.fold_in(key_of[9], 71), 0),
        "send_high": draw_send_high(jax.random.fold_in(key_of[9], 71), 0),
        "send_slot": draw_send_slot(jax.random.fold_in(key_of[9], 71), 0),
        "recv_slot": draw_recv_slot(jax.random.fold_in(key_of[9], 71), 0),
        "kernel": gaussian(key_of[6], (KVOL, C, C), (KVOL * C) ** -0.5, 0.109375, ((2, 4),)),
        "norm_gain": jnp.clip(1.0 + 0.1 * jax.random.normal(key_of[7], (C,), jnp.float32), 0.5, 1.5),
        "norm_shift": gaussian(key_of[8], (C,), 0.5, 3.0, (), jnp.float32),
    }


def gather_rows(table, index):
    return jnp.take(table, index, axis=0)

def convolve(extended, columns, kernel):

    def advance(summed, packed):
        column, weight_mat = packed
        picked = jnp.take(extended, column, axis=0)
        return (summed + jnp.dot(picked, weight_mat, preferred_element_type=jnp.float32), None)
    initial = jnp.zeros((columns.shape[1], kernel.shape[2]), jnp.float32)
    return lax.scan(advance, initial, (columns, kernel))[0]

def finish(conv_out, features, norm_gain, norm_shift):
    centered = conv_out - lax.optimization_barrier(jnp.mean(conv_out, axis=-1, keepdims=True))
    spread_sq = lax.optimization_barrier(jnp.mean(centered * centered, axis=-1, keepdims=True))
    normed = centered * lax.rsqrt(spread_sq + 1e-05) * norm_gain + norm_shift
    return (features.astype(jnp.float32) + jax.nn.silu(normed)).astype(jnp.bfloat16)

def reference(features, neighbors, send_low, send_high, send_slot, recv_slot, kernel, norm_gain, norm_shift):
    flat_bricks = features.reshape(BRICKS, V_DEV, C)
    bricked = features.reshape(N_BRICK, N_GRP, V_DEV, C)
    upward = jax.vmap(gather_rows)(flat_bricks, send_high.reshape(BRICKS, HALO)).reshape(N_BRICK, N_GRP, HALO, C)
    downward = jax.vmap(gather_rows)(flat_bricks, send_low.reshape(BRICKS, HALO)).reshape(N_BRICK, N_GRP, HALO, C)
    empty_slab = jnp.zeros((1, N_GRP, HALO, C), jnp.bfloat16)
    from_lower = jnp.concatenate([empty_slab, upward[:-1]], axis=0)
    from_upper = jnp.concatenate([downward[1:], empty_slab], axis=0)
    zero_rows = jnp.zeros((N_BRICK, N_GRP, 1, C), jnp.bfloat16)
    extended = jnp.concatenate([bricked, from_lower, from_upper, zero_rows], axis=2)
    extended = extended.reshape(BRICKS, V_DEV + 2 * HALO + 1, C)
    columns = neighbors.reshape(BRICKS, V_DEV, KVOL).transpose(0, 2, 1)

    def per_brick(packed):
        table, cols_here, feats = packed
        return finish(convolve(table, cols_here, kernel), feats, norm_gain, norm_shift)
    blended = lax.map(per_brick, (extended, columns, flat_bricks)).reshape(TOTAL, C)
    padded = jnp.concatenate([blended, jnp.zeros((1, C), jnp.bfloat16)], axis=0)
    carried = send_slot.reshape(N_BRICK, N_GRP, N_BRICK * CAP).astype(jnp.int32)
    slab_ids = jnp.arange(N_BRICK, dtype=jnp.int32)[:, None, None]
    group_ids = jnp.arange(N_GRP, dtype=jnp.int32)[None, :, None]
    wanted = recv_slot.reshape(N_BRICK, N_GRP, V_DEV).astype(jnp.int32)
    source = wanted // CAP
    column_pos = slab_ids * CAP + wanted % CAP
    groups = jnp.broadcast_to(group_ids, wanted.shape)
    local_row = carried[source, groups, column_pos]
    global_row = jnp.where(local_row < V_DEV, (source * N_GRP + groups) * V_DEV + local_row, TOTAL)
    return jnp.take(padded, global_row.reshape(TOTAL).astype(jnp.int32), axis=0)
```

```python
import functools

import jax
import jax.numpy as jnp
from jax import lax
from jax.experimental import pallas as pl
from jax.experimental.pallas import tpu as pltpu
from jax.sharding import PartitionSpec as P

BLOCK = 256


def shifted(block, axis, distance):
    devices = range(lax.axis_size(axis))
    route = [(i - distance, i) for i in devices if i - distance in devices]
    return lax.ppermute(block, axis, route)


def conv_kernel(
    nb_ref, feat_ref, low_ref, up_ref, w_ref, gain_ref, shift_ref, out_ref, tab_ref, buf_a, buf_b, acc_ref
):
    step = pl.program_id(0)
    rows, channels = feat_ref.shape
    halo = low_ref.shape[0]
    offsets, block = nb_ref.shape
    table = tab_ref.reshape(tab_ref.shape[0], 1, channels)

    @pl.when(step == 0)
    def _():
        chunk = 256
        for src, start in ((feat_ref, 0), (low_ref, rows), (up_ref, rows + halo)):

            @pl.loop(0, src.shape[0] // chunk)
            def _(i, src=src, start=start):
                at = pl.multiple_of(i * chunk, chunk)
                tab_ref[pl.ds(start + at, chunk), :] = src[pl.ds(at, chunk), :].astype(jnp.float32)

        tab_ref[pl.ds(rows + 2 * halo, 8), :] = jnp.zeros((8, channels), jnp.float32)

    def gather(first, buf, count=2):
        for j in range(count):
            for v in range(block):
                buf[pl.ds(v, 1), pl.ds(j * channels, channels)] = table[nb_ref[first + j, v]]

    def multiply(first, buf, count=2):
        lhs = buf[:, : count * channels].astype(jnp.bfloat16)
        at = pl.multiple_of(first * channels, channels)
        rhs = w_ref[pl.ds(at, count * channels), :]
        acc_ref[...] += jnp.dot(lhs, rhs, preferred_element_type=jnp.float32)

    acc_ref[...] = jnp.zeros_like(acc_ref)
    pairs = offsets // 2
    gather(0, buf_a)

    @pl.loop(0, (pairs - 1) // 2)
    def _(p):
        first = p * 4
        gather(first + 2, buf_b)
        multiply(first, buf_a)
        gather(first + 4, buf_a)
        multiply(first + 2, buf_b)

    gather(offsets - 1, buf_b, 1)
    multiply(offsets - 3, buf_a)
    multiply(offsets - 1, buf_b, 1)

    summed = acc_ref[...]
    centered = summed - jnp.mean(summed, axis=-1, keepdims=True)
    spread_sq = jnp.mean(centered * centered, axis=-1, keepdims=True)
    normed = centered * lax.rsqrt(spread_sq + 1e-05) * gain_ref[...] + shift_ref[...]
    own = feat_ref[pl.ds(pl.multiple_of(step * block, block), block), :].astype(jnp.float32)
    out_ref[...] = (own + normed / (1.0 + jnp.exp(-normed))).astype(jnp.bfloat16)


def conv_block(features, from_lower, from_upper, columns, weights, gain, shift):
    rows, channels = features.shape
    halo = from_lower.shape[0]
    offsets = columns.shape[0]
    block = BLOCK
    whole = pl.BlockSpec(memory_space=pltpu.VMEM)
    return pl.pallas_call(
        conv_kernel,
        grid=(rows // block,),
        out_shape=jax.ShapeDtypeStruct((rows, channels), jnp.bfloat16),
        in_specs=[
            pl.BlockSpec((offsets, block), lambda i: (0, i), memory_space=pltpu.SMEM),
            whole,
            whole,
            whole,
            whole,
            whole,
            whole,
        ],
        out_specs=pl.BlockSpec((block, channels), lambda i: (i, 0)),
        scratch_shapes=[
            pltpu.VMEM((rows + 2 * halo + 8, channels), jnp.float32),
            pltpu.VMEM((block, 2 * channels), jnp.float32),
            pltpu.VMEM((block, 2 * channels), jnp.float32),
            pltpu.VMEM((block, channels), jnp.float32),
        ],
        compiler_params=pltpu.CompilerParams(vmem_limit_bytes=48 * 1024 * 1024),
        cost_estimate=pl.CostEstimate(
            flops=2 * rows * offsets * channels * channels,
            bytes_accessed=8 * rows * channels,
            transcendentals=rows * channels,
        ),
    )(columns, features, from_lower, from_upper, weights, gain, shift)


def body(
    features, neighbors, send_low, send_high, send_slot, recv_slot, kernel, norm_gain, norm_shift
):
    row_count, channels = features.shape
    zero_row = jnp.zeros((1, channels), jnp.bfloat16)
    weights = lax.all_gather(kernel, "grp", axis=2, tiled=True)
    upward = jnp.take(features, send_high, axis=0)
    downward = jnp.take(features, send_low, axis=0)
    from_lower = shifted(upward, "brick", 1)
    from_upper = shifted(downward, "brick", -1)
    blended = conv_block(
        features,
        from_lower,
        from_upper,
        neighbors.T,
        weights.reshape(-1, channels),
        norm_gain.reshape(1, channels),
        norm_shift.reshape(1, channels),
    )
    slab_count = lax.axis_size("brick")
    capacity = send_slot.shape[0] // slab_count
    padded = jnp.concatenate([blended, zero_row], axis=0)
    outbox = jnp.take(padded, send_slot, axis=0)
    arrived = lax.all_to_all(
        outbox.reshape(slab_count, capacity, channels),
        "brick",
        split_axis=0,
        concat_axis=0,
        tiled=True,
    )
    return jnp.take(arrived.reshape(slab_count * capacity, channels), recv_slot, axis=0)


def solution(mesh):
    return jax.shard_map(
        body,
        mesh=mesh,
        in_specs=(
            P(("brick", "grp"), None),
            P(("brick", "grp"), None),
            P(("brick", "grp")),
            P(("brick", "grp")),
            P(("brick", "grp")),
            P(("brick", "grp")),
            P(None, None, "grp"),
            P(),
            P(),
        ),
        out_specs=P(("brick", "grp"), None),
        check_vma=False,
    )
```

```python
import functools

import jax
import jax.numpy as jnp
from jax import lax
from jax.experimental import pallas as pl
from jax.experimental.pallas import tpu as pltpu
from jax.sharding import PartitionSpec as P

BLOCK = 256


def shifted(block, axis, distance):
    devices = range(lax.axis_size(axis))
    route = [(i - distance, i) for i in devices if i - distance in devices]
    return lax.ppermute(block, axis, route)


def compact_kernel(nb_ref, list_ref, pos_ref, *, absent):
    offsets, block = nb_ref.shape
    value = nb_ref[...]
    present = value != absent
    lane = lax.broadcasted_iota(jnp.int32, (offsets, block), 1)
    before = lax.broadcasted_iota(jnp.int32, (block, block), 0)
    after = lax.broadcasted_iota(jnp.int32, (block, block), 1)
    triangle = jnp.where(before <= after, 1.0, 0.0).astype(jnp.bfloat16)
    ones = jnp.where(present, 1.0, 0.0).astype(jnp.bfloat16)
    counted = jnp.dot(ones, triangle, preferred_element_type=jnp.float32).astype(jnp.int32)
    pos = counted - 1
    pos_ref[...] = jnp.where(present, pos, -1)
    word = jnp.where(present, value + (lane - pos) * 16384 + (1 << 23), 0)
    for bit in range(block.bit_length() - 1):
        moves = (word & (16384 << bit)) != 0
        moved = pltpu.roll(jnp.where(moves, word, 0), block - (1 << bit), 1)
        word = jnp.where(moves, 0, word) + moved
    list_ref[...] = jnp.where(word != 0, word & 16383, absent)


def conv_kernel(
    list_ref,
    pos_ref,
    feat_ref,
    low_ref,
    up_ref,
    w_ref,
    gain_ref,
    shift_ref,
    out_ref,
    tab_ref,
    buf_a,
    buf_b,
    acc_ref,
):
    step = pl.program_id(0)
    rows, channels = feat_ref.shape
    halo = low_ref.shape[0]
    offsets, block = list_ref.shape
    half = block // 2
    middle = offsets // 2
    absent = rows + 2 * halo
    table = tab_ref.reshape(tab_ref.shape[0], 1, channels)
    slots = lax.broadcasted_iota(jnp.int32, (half, block), 0)

    @pl.when(step == 0)
    def _():
        chunk = 256
        for src, start in ((feat_ref, 0), (low_ref, rows), (up_ref, rows + halo)):

            @pl.loop(0, src.shape[0] // chunk)
            def _(i, src=src, start=start):
                at = pl.multiple_of(i * chunk, chunk)
                tab_ref[pl.ds(start + at, chunk), :] = src[pl.ds(at, chunk), :].astype(jnp.float32)

        tab_ref[pl.ds(absent, 8), :] = jnp.zeros((8, channels), jnp.float32)

    def offset_of(pair, j):
        at = 2 * pair + j
        return at + jnp.where(at >= middle, 1, 0)

    def gather(pair, buf, base=0):
        for j in range(2):
            k = offset_of(pair, j)
            for c in range(half):
                buf[pl.ds(j * half + c, 1), :] = table[list_ref[k, base + c]]

    def multiply(pair, buf, base=0):
        products, spreads = [], []
        for j in range(2):
            k = offset_of(pair, j)
            rows_in = buf[j * half : (j + 1) * half, :].astype(jnp.bfloat16)
            products.append(
                lax.dot_general(
                    w_ref[k], rows_in, (((1,), (1,)), ((), ())), preferred_element_type=jnp.float32
                )
            )
            wanted = pos_ref[pl.ds(k, 1), :] - base
            spreads.append(jnp.where(slots == wanted, 1.0, 0.0).astype(jnp.bfloat16))
        product = jnp.concatenate(products, axis=1)
        high = product.astype(jnp.bfloat16)
        low = (product - high.astype(jnp.float32)).astype(jnp.bfloat16)
        both = jnp.concatenate([high, low], axis=0)
        spread = jnp.concatenate(spreads, axis=0)
        result = jnp.dot(both, spread, preferred_element_type=jnp.float32)
        acc_ref[...] += result[:channels] + result[channels:]

    own = feat_ref[pl.ds(pl.multiple_of(step * block, block), block), :]
    gather(0, buf_a)
    acc_ref[...] = lax.dot_general(
        w_ref[middle], own, (((1,), (1,)), ((), ())), preferred_element_type=jnp.float32
    )

    pairs = middle

    @pl.loop(0, pairs // 2)
    def _(p):
        first = 2 * p
        gather(first + 1, buf_b)
        multiply(first, buf_a)
        gather(first + 2, buf_a)
        multiply(first + 1, buf_b)

    multiply(pairs - 1, buf_a)

    crowded = jnp.int32(0)
    for k in range(offsets):
        if k != middle:
            crowded = crowded + jnp.where(list_ref[k, half] != absent, 1, 0)

    @pl.when(crowded > 0)
    def _():

        @pl.loop(0, pairs)
        def _(p):
            more = (list_ref[offset_of(p, 0), half] != absent) | (
                list_ref[offset_of(p, 1), half] != absent
            )

            @pl.when(more)
            def _():
                gather(p, buf_a, half)
                multiply(p, buf_a, half)

    summed = acc_ref[...].T
    centered = summed - jnp.mean(summed, axis=-1, keepdims=True)
    spread_sq = jnp.mean(centered * centered, axis=-1, keepdims=True)
    normed = centered * lax.rsqrt(spread_sq + 1e-05) * gain_ref[...] + shift_ref[...]
    blended = own.astype(jnp.float32) + normed / (1.0 + jnp.exp(-normed))
    out_ref[...] = blended.astype(jnp.bfloat16)


def compact(columns, absent):
    offsets, rows = columns.shape
    spec = pl.BlockSpec((offsets, BLOCK), lambda i: (0, i))
    shape = jax.ShapeDtypeStruct((offsets, rows), jnp.int32)
    return pl.pallas_call(
        functools.partial(compact_kernel, absent=absent),
        grid=(rows // BLOCK,),
        out_shape=(shape, shape),
        in_specs=[spec],
        out_specs=(spec, spec),
        cost_estimate=pl.CostEstimate(
            flops=100 * rows * offsets, bytes_accessed=12 * rows * offsets, transcendentals=0
        ),
    )(columns)


def conv_block(features, from_lower, from_upper, lists, places, weights, gain, shift):
    rows, channels = features.shape
    halo = from_lower.shape[0]
    offsets = lists.shape[0]
    block = BLOCK
    whole = pl.BlockSpec(memory_space=pltpu.VMEM)
    return pl.pallas_call(
        conv_kernel,
        grid=(rows // block,),
        out_shape=jax.ShapeDtypeStruct((rows, channels), jnp.bfloat16),
        in_specs=[
            pl.BlockSpec((offsets, block), lambda i: (0, i), memory_space=pltpu.SMEM),
            pl.BlockSpec((offsets, block), lambda i: (0, i)),
            whole,
            whole,
            whole,
            whole,
            whole,
            whole,
        ],
        out_specs=pl.BlockSpec((block, channels), lambda i: (i, 0)),
        scratch_shapes=[
            pltpu.VMEM((rows + 2 * halo + 8, channels), jnp.float32),
            pltpu.VMEM((block, channels), jnp.float32),
            pltpu.VMEM((block, channels), jnp.float32),
            pltpu.VMEM((channels, block), jnp.float32),
        ],
        compiler_params=pltpu.CompilerParams(vmem_limit_bytes=48 * 1024 * 1024),
        cost_estimate=pl.CostEstimate(
            flops=2 * rows * offsets * channels * channels,
            bytes_accessed=8 * rows * channels,
            transcendentals=rows * channels,
        ),
    )(lists, places, features, from_lower, from_upper, weights, gain, shift)


def body(
    features, neighbors, send_low, send_high, send_slot, recv_slot, kernel, norm_gain, norm_shift
):
    row_count, channels = features.shape
    zero_row = jnp.zeros((1, channels), jnp.bfloat16)
    weights = lax.all_gather(kernel.transpose(0, 2, 1), "grp", axis=1, tiled=True)
    upward = jnp.take(features, send_high, axis=0)
    downward = jnp.take(features, send_low, axis=0)
    from_lower = shifted(upward, "brick", 1)
    from_upper = shifted(downward, "brick", -1)
    lists, places = compact(neighbors.T, row_count + 2 * send_low.shape[0])
    blended = conv_block(
        features,
        from_lower,
        from_upper,
        lists,
        places,
        weights,
        norm_gain.reshape(1, channels),
        norm_shift.reshape(1, channels),
    )
    slab_count = lax.axis_size("brick")
    capacity = send_slot.shape[0] // slab_count
    padded = jnp.concatenate([blended, zero_row], axis=0)
    outbox = jnp.take(padded, send_slot, axis=0)
    arrived = lax.all_to_all(
        outbox.reshape(slab_count, capacity, channels),
        "brick",
        split_axis=0,
        concat_axis=0,
        tiled=True,
    )
    return jnp.take(arrived.reshape(slab_count * capacity, channels), recv_slot, axis=0)


def solution(mesh):
    return jax.shard_map(
        body,
        mesh=mesh,
        in_specs=(
            P(("brick", "grp"), None),
            P(("brick", "grp"), None),
            P(("brick", "grp")),
            P(("brick", "grp")),
            P(("brick", "grp")),
            P(("brick", "grp")),
            P(None, None, "grp"),
            P(),
            P(),
        ),
        out_specs=P(("brick", "grp"), None),
        check_vma=False,
    )
```

```python
import functools

import jax
import jax.numpy as jnp
from jax import lax
from jax.experimental import pallas as pl
from jax.experimental.pallas import tpu as pltpu
from jax.sharding import PartitionSpec as P

BLOCK = 256


def shifted(block, axis, distance):
    devices = range(lax.axis_size(axis))
    route = [(i - distance, i) for i in devices if i - distance in devices]
    return lax.ppermute(block, axis, route)


def compact_kernel(nb_ref, list_ref, pos_ref, *, absent):
    offsets, block = nb_ref.shape
    value = nb_ref[...]
    present = value != absent
    lane = lax.broadcasted_iota(jnp.int32, (offsets, block), 1)
    before = lax.broadcasted_iota(jnp.int32, (block, block), 0)
    after = lax.broadcasted_iota(jnp.int32, (block, block), 1)
    triangle = jnp.where(before <= after, 1.0, 0.0).astype(jnp.bfloat16)
    ones = jnp.where(present, 1.0, 0.0).astype(jnp.bfloat16)
    counted = jnp.dot(ones, triangle, preferred_element_type=jnp.float32).astype(jnp.int32)
    pos = counted - 1
    pos_ref[...] = jnp.where(present, pos, -1)
    word = jnp.where(present, value + (lane - pos) * 16384 + (1 << 23), 0)
    for bit in range(block.bit_length() - 1):
        moves = (word & (16384 << bit)) != 0
        moved = pltpu.roll(jnp.where(moves, word, 0), block - (1 << bit), 1)
        word = jnp.where(moves, 0, word) + moved
    list_ref[...] = jnp.where(word != 0, word & 16383, absent)


def conv_kernel(
    list_ref,
    pos_ref,
    feat_ref,
    low_ref,
    up_ref,
    w_ref,
    gain_ref,
    shift_ref,
    out_ref,
    tab_ref,
    buf_a,
    buf_b,
    acc_ref,
):
    step = pl.program_id(0)
    rows, channels = feat_ref.shape
    halo = low_ref.shape[0]
    offsets, block = list_ref.shape
    half = block // 2
    middle = offsets // 2
    absent = rows + 2 * halo
    table = tab_ref.reshape(tab_ref.shape[0], 1, channels)
    slots = lax.broadcasted_iota(jnp.int32, (half, block), 0)

    @pl.when(step == 0)
    def _():
        chunk = 256
        for src, start in ((feat_ref, 0), (low_ref, rows), (up_ref, rows + halo)):

            @pl.loop(0, src.shape[0] // chunk)
            def _(i, src=src, start=start):
                at = pl.multiple_of(i * chunk, chunk)
                tab_ref[pl.ds(start + at, chunk), :] = src[pl.ds(at, chunk), :].astype(jnp.float32)

        tab_ref[pl.ds(absent, 8), :] = jnp.zeros((8, channels), jnp.float32)

    def offset_of(pair, j):
        at = 2 * pair + j
        return at + jnp.where(at >= middle, 1, 0)

    def gather(pair, buf, base=0):
        for j in range(2):
            k = offset_of(pair, j)
            for c in range(half):
                buf[pl.ds(j * half + c, 1), :] = table[list_ref[k, base + c]]

    def multiply(pair, buf, base=0):
        products, spreads = [], []
        for j in range(2):
            k = offset_of(pair, j)
            rows_in = buf[j * half : (j + 1) * half, :].astype(jnp.bfloat16)
            products.append(
                lax.dot_general(
                    w_ref[k], rows_in, (((1,), (1,)), ((), ())), preferred_element_type=jnp.float32
                )
            )
            wanted = pos_ref[pl.ds(k, 1), :] - base
            spreads.append(jnp.where(slots == wanted, 1.0, 0.0).astype(jnp.bfloat16))
        product = jnp.concatenate(products, axis=1)
        high = product.astype(jnp.bfloat16)
        low = (product - high.astype(jnp.float32)).astype(jnp.bfloat16)
        both = jnp.concatenate([high, low], axis=0)
        spread = jnp.concatenate(spreads, axis=0)
        result = jnp.dot(both, spread, preferred_element_type=jnp.float32)
        acc_ref[...] += result[:channels] + result[channels:]

    own = feat_ref[pl.ds(pl.multiple_of(step * block, block), block), :]
    gather(0, buf_a)
    acc_ref[...] = lax.dot_general(
        w_ref[middle], own, (((1,), (1,)), ((), ())), preferred_element_type=jnp.float32
    )

    pairs = middle

    @pl.loop(0, pairs // 2)
    def _(p):
        first = 2 * p
        gather(first + 1, buf_b)
        multiply(first, buf_a)
        gather(first + 2, buf_a)
        multiply(first + 1, buf_b)

    multiply(pairs - 1, buf_a)

    crowded = jnp.int32(0)
    for k in range(offsets):
        if k != middle:
            crowded = crowded + jnp.where(list_ref[k, half] != absent, 1, 0)

    @pl.when(crowded > 0)
    def _():

        @pl.loop(0, pairs)
        def _(p):
            more = (list_ref[offset_of(p, 0), half] != absent) | (
                list_ref[offset_of(p, 1), half] != absent
            )

            @pl.when(more)
            def _():
                gather(p, buf_a, half)
                multiply(p, buf_a, half)

    summed = acc_ref[...].T
    centered = summed - jnp.mean(summed, axis=-1, keepdims=True)
    spread_sq = jnp.mean(centered * centered, axis=-1, keepdims=True)
    normed = centered * lax.rsqrt(spread_sq + 1e-05) * gain_ref[...] + shift_ref[...]
    blended = own.astype(jnp.float32) + normed / (1.0 + jnp.exp(-normed))
    out_ref[...] = blended.astype(jnp.bfloat16)


def compact(columns, absent):
    offsets, rows = columns.shape
    spec = pl.BlockSpec((offsets, BLOCK), lambda i: (0, i))
    shape = jax.ShapeDtypeStruct((offsets, rows), jnp.int32)
    return pl.pallas_call(
        functools.partial(compact_kernel, absent=absent),
        grid=(rows // BLOCK,),
        out_shape=(shape, shape),
        in_specs=[spec],
        out_specs=(spec, spec),
        cost_estimate=pl.CostEstimate(
            flops=100 * rows * offsets, bytes_accessed=12 * rows * offsets, transcendentals=0
        ),
    )(columns)


def conv_block(features, from_lower, from_upper, lists, places, weights, gain, shift):
    rows, channels = features.shape
    halo = from_lower.shape[0]
    offsets = lists.shape[0]
    block = BLOCK
    whole = pl.BlockSpec(memory_space=pltpu.VMEM)
    return pl.pallas_call(
        conv_kernel,
        grid=(rows // block,),
        out_shape=jax.ShapeDtypeStruct((rows, channels), jnp.bfloat16),
        in_specs=[
            pl.BlockSpec((offsets, block), lambda i: (0, i), memory_space=pltpu.SMEM),
            pl.BlockSpec((offsets, block), lambda i: (0, i)),
            whole,
            whole,
            whole,
            whole,
            whole,
            whole,
        ],
        out_specs=pl.BlockSpec((block, channels), lambda i: (i, 0)),
        scratch_shapes=[
            pltpu.VMEM((rows + 2 * halo + 8, channels), jnp.float32),
            pltpu.VMEM((block, channels), jnp.float32),
            pltpu.VMEM((block, channels), jnp.float32),
            pltpu.VMEM((channels, block), jnp.float32),
        ],
        compiler_params=pltpu.CompilerParams(vmem_limit_bytes=48 * 1024 * 1024),
        cost_estimate=pl.CostEstimate(
            flops=2 * rows * offsets * channels * channels,
            bytes_accessed=8 * rows * channels,
            transcendentals=rows * channels,
        ),
    )(lists, places, features, from_lower, from_upper, weights, gain, shift)


def relay_kernel(
    send_ref,
    recv_ref,
    rows_ref,
    out_ref,
    table_ref,
    stage_ref,
    outbox_ref,
    inbox_ref,
    arrived_ref,
    send_sem,
    recv_sem,
    *,
    axis,
    count,
):
    me = lax.axis_index(axis)
    rows, channels = rows_ref.shape
    capacity = outbox_ref.shape[1]
    chunk = stage_ref.shape[0]
    table = table_ref.reshape(table_ref.shape[0], 1, channels)
    arrived = arrived_ref.reshape(arrived_ref.shape[0], 1, channels)

    barrier = pltpu.get_barrier_semaphore()

    @pl.loop(1, count)
    def _(j):
        pl.semaphore_signal(
            barrier,
            inc=1,
            device_id={axis: lax.rem(me + j, count)},
            device_id_type=pl.DeviceIdType.MESH,
        )

    @pl.loop(0, rows // chunk)
    def _(i):
        at = pl.ds(pl.multiple_of(i * chunk, chunk), chunk)
        table_ref[at, :] = rows_ref[at, :].astype(jnp.float32)

    table_ref[pl.ds(rows, 8), :] = jnp.zeros((8, channels), jnp.float32)
    pl.semaphore_wait(barrier, count - 1)

    def copy_to(j):
        to = lax.rem(me + j, count)
        return pltpu.make_async_remote_copy(
            src_ref=outbox_ref.at[to],
            dst_ref=inbox_ref.at[me],
            send_sem=send_sem.at[j],
            recv_sem=recv_sem.at[j],
            device_id={axis: to},
            device_id_type=pl.DeviceIdType.MESH,
        )

    def fill(shard, into_ref):
        @pl.loop(0, capacity // chunk)
        def _(i):
            first = pl.multiple_of(i * chunk, chunk)
            for c in range(chunk):
                stage_ref[pl.ds(c, 1), :] = table[send_ref[shard * capacity + first + c]]
            into_ref[pl.ds(first, chunk), :] = stage_ref[...].astype(jnp.bfloat16)

    @pl.loop(0, count - 1)
    def _(i):
        j = lax.rem(i + count // 2, count - 1) + 1
        fill(lax.rem(me + j, count), outbox_ref.at[lax.rem(me + j, count)])
        copy_to(j).start()

    fill(me, inbox_ref.at[me])

    def widen(source):
        @pl.loop(0, capacity // chunk)
        def _(i):
            first = pl.multiple_of(i * chunk, chunk)
            to = pl.multiple_of(source * capacity + first, chunk)
            arrived_ref[pl.ds(to, chunk), :] = inbox_ref[source, pl.ds(first, chunk), :].astype(
                jnp.float32
            )

    widen(me)

    @pl.loop(0, count - 1)
    def _(i):
        j = lax.rem(i + count // 2, count - 1) + 1
        source = lax.rem(me - j + count, count)
        pltpu.make_async_remote_copy(
            src_ref=outbox_ref.at[source],
            dst_ref=inbox_ref.at[source],
            send_sem=send_sem.at[j],
            recv_sem=recv_sem.at[j],
            device_id={axis: source},
            device_id_type=pl.DeviceIdType.MESH,
        ).wait_recv()
        widen(source)

    @pl.loop(0, rows // chunk)
    def _(i):
        first = pl.multiple_of(i * chunk, chunk)
        for c in range(chunk):
            stage_ref[pl.ds(c, 1), :] = arrived[recv_ref[first + c]]
        out_ref[pl.ds(first, chunk), :] = stage_ref[...].astype(jnp.bfloat16)

    @pl.loop(1, count)
    def _(j):
        copy_to(j).wait_send()


def relay(blended, send_slot, recv_slot, axis):
    rows, channels = blended.shape
    count = lax.axis_size(axis)
    capacity = send_slot.shape[0] // count
    chunk = 128
    whole = pl.BlockSpec(memory_space=pltpu.VMEM)
    scalars = pl.BlockSpec(memory_space=pltpu.SMEM)
    boxes = pltpu.VMEM((count, capacity, channels), jnp.bfloat16)
    return pl.pallas_call(
        functools.partial(relay_kernel, axis=axis, count=count),
        out_shape=jax.ShapeDtypeStruct((rows, channels), jnp.bfloat16),
        in_specs=[scalars, scalars, whole],
        out_specs=whole,
        scratch_shapes=[
            pltpu.VMEM((rows + 8, channels), jnp.float32),
            pltpu.VMEM((chunk, channels), jnp.float32),
            boxes,
            boxes,
            pltpu.VMEM((count * capacity, channels), jnp.float32),
            pltpu.SemaphoreType.DMA((count,)),
            pltpu.SemaphoreType.DMA((count,)),
        ],
        compiler_params=pltpu.CompilerParams(
            collective_id=0, has_side_effects=True, vmem_limit_bytes=48 * 1024 * 1024
        ),
    )(send_slot, recv_slot, blended)


def body(
    features, neighbors, send_low, send_high, send_slot, recv_slot, kernel, norm_gain, norm_shift
):
    row_count, channels = features.shape
    weights = lax.all_gather(kernel.transpose(0, 2, 1), "grp", axis=1, tiled=True)
    upward = jnp.take(features, send_high, axis=0)
    downward = jnp.take(features, send_low, axis=0)
    from_lower = shifted(upward, "brick", 1)
    from_upper = shifted(downward, "brick", -1)
    lists, places = compact(neighbors.T, row_count + 2 * send_low.shape[0])
    blended = conv_block(
        features,
        from_lower,
        from_upper,
        lists,
        places,
        weights,
        norm_gain.reshape(1, channels),
        norm_shift.reshape(1, channels),
    )
    return relay(blended, send_slot, recv_slot, "brick")


def solution(mesh):
    return jax.shard_map(
        body,
        mesh=mesh,
        in_specs=(
            P(("brick", "grp"), None),
            P(("brick", "grp"), None),
            P(("brick", "grp")),
            P(("brick", "grp")),
            P(("brick", "grp")),
            P(("brick", "grp")),
            P(None, None, "grp"),
            P(),
            P(),
        ),
        out_specs=P(("brick", "grp"), None),
        check_vma=False,
    )
```

```python
import functools

import jax
import jax.numpy as jnp
from jax import lax
from jax.experimental import pallas as pl
from jax.experimental.pallas import tpu as pltpu
from jax.sharding import PartitionSpec as P

BLOCK = 256


def shifted(block, axis, distance):
    devices = range(lax.axis_size(axis))
    route = [(i - distance, i) for i in devices if i - distance in devices]
    return lax.ppermute(block, axis, route)


def compact_kernel(nb_ref, list_ref, pos_ref, *, absent, block):
    offsets, width = nb_ref.shape
    value = nb_ref[...]
    present = value != absent
    lane = lax.broadcasted_iota(jnp.int32, (offsets, width), 1) & (block - 1)
    before = lax.broadcasted_iota(jnp.int32, (block, block), 0)
    after = lax.broadcasted_iota(jnp.int32, (block, block), 1)
    triangle = jnp.where(before <= after, 1.0, 0.0).astype(jnp.bfloat16)
    ones = jnp.where(present, 1.0, 0.0).astype(jnp.bfloat16)
    counted = [
        jnp.dot(ones[:, at : at + block], triangle, preferred_element_type=jnp.float32)
        for at in range(0, width, block)
    ]
    pos = jnp.concatenate(counted, axis=1).astype(jnp.int32) - 1
    pos_ref[...] = jnp.where(present, pos, -1)
    word = jnp.where(present, value + (lane - pos) * 16384 + (1 << 23), 0)
    for bit in range(block.bit_length() - 1):
        moves = (word & (16384 << bit)) != 0
        moved = pltpu.roll(jnp.where(moves, word, 0), width - (1 << bit), 1)
        word = jnp.where(moves, 0, word) + moved
    list_ref[...] = jnp.where(word != 0, word & 16383, absent)


def conv_kernel(
    list_ref,
    next_ref,
    pos_ref,
    feat_ref,
    low_ref,
    up_ref,
    w_ref,
    gain_ref,
    shift_ref,
    out_ref,
    tab_ref,
    buf_a,
    buf_b,
    acc_ref,
):
    step = pl.program_id(0)
    rows, channels = feat_ref.shape
    halo = low_ref.shape[0]
    offsets, block = list_ref.shape
    half = block // 2
    middle = offsets // 2
    absent = rows + 2 * halo
    table = tab_ref.reshape(tab_ref.shape[0], 1, channels)
    slots = lax.broadcasted_iota(jnp.int32, (half, block), 0)

    @pl.when(step == 0)
    def _():
        chunk = 256
        for src, start in ((feat_ref, 0), (low_ref, rows), (up_ref, rows + halo)):

            @pl.loop(0, src.shape[0] // chunk)
            def _(i, src=src, start=start):
                at = pl.multiple_of(i * chunk, chunk)
                tab_ref[pl.ds(start + at, chunk), :] = src[pl.ds(at, chunk), :].astype(jnp.float32)

        tab_ref[pl.ds(absent, 8), :] = jnp.zeros((8, channels), jnp.float32)

    def offset_of(pair, j):
        at = 2 * pair + j
        return at + jnp.where(at >= middle, 1, 0)

    def gather(pair, buf, base=0, count=2, lists=list_ref):
        for j in range(2 * count):
            k = offset_of(pair, j)
            for c in range(half):
                buf[pl.ds(j * half + c, 1), :] = table[lists[k, base + c]]

    def multiply(pair, buf, base=0, count=2):
        total = jnp.zeros_like(acc_ref)
        for i in range(count):
            products, spreads = [], []
            for j in range(2 * i, 2 * i + 2):
                k = offset_of(pair, j)
                rows_in = buf[j * half : (j + 1) * half, :].astype(jnp.bfloat16)
                products.append(
                    lax.dot_general(
                        w_ref[k],
                        rows_in,
                        (((1,), (1,)), ((), ())),
                        preferred_element_type=jnp.float32,
                    )
                )
                wanted = pos_ref[pl.ds(k, 1), :] - base
                spreads.append(jnp.where(slots == wanted, 1.0, 0.0).astype(jnp.bfloat16))
            product = jnp.concatenate(products, axis=1)
            high = product.astype(jnp.bfloat16)
            low = (product - high.astype(jnp.float32)).astype(jnp.bfloat16)
            both = jnp.concatenate([high, low], axis=0)
            spread = jnp.concatenate(spreads, axis=0)
            result = jnp.dot(both, spread, preferred_element_type=jnp.float32)
            total += result[:channels] + result[channels:]
        acc_ref[...] += total

    own = feat_ref[pl.ds(pl.multiple_of(step * block, block), block), :]
    pairs = middle

    @pl.when(step == 0)
    def _():
        gather(0, buf_a, count=1)

    acc_ref[...] = lax.dot_general(
        w_ref[middle], own, (((1,), (1,)), ((), ())), preferred_element_type=jnp.float32
    )
    gather(1, buf_b)
    multiply(0, buf_a, count=1)

    @pl.loop(0, (pairs - 3) // 4)
    def _(p):
        first = 1 + 4 * p
        gather(first + 2, buf_a)
        multiply(first, buf_b)
        gather(first + 4, buf_b)
        multiply(first + 2, buf_a)

    gather(pairs - 2, buf_a)
    multiply(pairs - 4, buf_b)

    crowded = jnp.int32(0)
    for k in range(offsets):
        if k != middle:
            crowded = crowded + jnp.where(list_ref[k, half] != absent, 1, 0)

    @pl.when(crowded > 0)
    def _():

        @pl.loop(0, pairs)
        def _(p):
            more = (list_ref[offset_of(p, 0), half] != absent) | (
                list_ref[offset_of(p, 1), half] != absent
            )

            @pl.when(more)
            def _():
                gather(p, buf_b, half, 1)
                multiply(p, buf_b, half, 1)

    multiply(pairs - 2, buf_a)
    gather(0, buf_a, count=1, lists=next_ref)
    summed = acc_ref[...].T
    centered = summed - jnp.mean(summed, axis=-1, keepdims=True)
    spread_sq = jnp.mean(centered * centered, axis=-1, keepdims=True)
    normed = centered * lax.rsqrt(spread_sq + 1e-05) * gain_ref[...] + shift_ref[...]
    blended = own.astype(jnp.float32) + normed / (1.0 + jnp.exp(-normed))
    out_ref[...] = blended.astype(jnp.bfloat16)


def compact(columns, absent):
    offsets, rows = columns.shape
    width = 8 * BLOCK
    spec = pl.BlockSpec((offsets, width), lambda i: (0, i))
    shape = jax.ShapeDtypeStruct((offsets, rows), jnp.int32)
    return pl.pallas_call(
        functools.partial(compact_kernel, absent=absent, block=BLOCK),
        grid=(rows // width,),
        out_shape=(shape, shape),
        in_specs=[spec],
        out_specs=(spec, spec),
        cost_estimate=pl.CostEstimate(
            flops=0, bytes_accessed=200 * rows * offsets, transcendentals=0
        ),
    )(columns)


def conv_block(features, from_lower, from_upper, lists, places, weights, gain, shift):
    rows, channels = features.shape
    halo = from_lower.shape[0]
    offsets = lists.shape[0]
    block = BLOCK
    whole = pl.BlockSpec(memory_space=pltpu.VMEM)
    last = rows // block - 1
    return pl.pallas_call(
        conv_kernel,
        grid=(rows // block,),
        out_shape=jax.ShapeDtypeStruct((rows, channels), jnp.bfloat16),
        in_specs=[
            pl.BlockSpec((offsets, block), lambda i: (0, i), memory_space=pltpu.SMEM),
            pl.BlockSpec(
                (offsets, block), lambda i: (0, jnp.minimum(i + 1, last)), memory_space=pltpu.SMEM
            ),
            pl.BlockSpec((offsets, block), lambda i: (0, i)),
            whole,
            whole,
            whole,
            whole,
            whole,
            whole,
        ],
        out_specs=pl.BlockSpec((block, channels), lambda i: (i, 0)),
        scratch_shapes=[
            pltpu.VMEM((rows + 2 * halo + 8, channels), jnp.float32),
            pltpu.VMEM((2 * block, channels), jnp.float32),
            pltpu.VMEM((2 * block, channels), jnp.float32),
            pltpu.VMEM((channels, block), jnp.float32),
        ],
        compiler_params=pltpu.CompilerParams(vmem_limit_bytes=48 * 1024 * 1024),
        cost_estimate=pl.CostEstimate(
            flops=2 * rows * offsets * channels * channels,
            bytes_accessed=8 * rows * channels,
            transcendentals=rows * channels,
        ),
    )(lists, lists, places, features, from_lower, from_upper, weights, gain, shift)


def relay_kernel(
    send_ref,
    recv_ref,
    rows_ref,
    out_ref,
    table_ref,
    stage_ref,
    outbox_ref,
    inbox_ref,
    arrived_ref,
    send_sem,
    recv_sem,
    *,
    axis,
    count,
):
    me = lax.axis_index(axis)
    rows, channels = rows_ref.shape
    capacity = outbox_ref.shape[1]
    chunk = stage_ref.shape[0]
    table = table_ref.reshape(table_ref.shape[0], 1, channels)
    arrived = arrived_ref.reshape(arrived_ref.shape[0], 1, channels)

    barrier = pltpu.get_barrier_semaphore()

    @pl.loop(1, count)
    def _(j):
        pl.semaphore_signal(
            barrier,
            inc=1,
            device_id={axis: lax.rem(me + j, count)},
            device_id_type=pl.DeviceIdType.MESH,
        )

    @pl.loop(0, rows // chunk)
    def _(i):
        at = pl.ds(pl.multiple_of(i * chunk, chunk), chunk)
        table_ref[at, :] = rows_ref[at, :].astype(jnp.float32)

    table_ref[pl.ds(rows, 8), :] = jnp.zeros((8, channels), jnp.float32)
    pl.semaphore_wait(barrier, count - 1)

    def copy_to(j):
        to = lax.rem(me + j, count)
        return pltpu.make_async_remote_copy(
            src_ref=outbox_ref.at[to],
            dst_ref=inbox_ref.at[me],
            send_sem=send_sem.at[j],
            recv_sem=recv_sem.at[j],
            device_id={axis: to},
            device_id_type=pl.DeviceIdType.MESH,
        )

    def fill(shard, into_ref):
        @pl.loop(0, capacity // chunk)
        def _(i):
            first = pl.multiple_of(i * chunk, chunk)
            for c in range(chunk):
                stage_ref[pl.ds(c, 1), :] = table[send_ref[shard * capacity + first + c]]
            into_ref[pl.ds(first, chunk), :] = stage_ref[...].astype(jnp.bfloat16)

    @pl.loop(0, count - 1)
    def _(i):
        j = lax.rem(i + count // 2, count - 1) + 1
        fill(lax.rem(me + j, count), outbox_ref.at[lax.rem(me + j, count)])
        copy_to(j).start()

    fill(me, inbox_ref.at[me])

    def widen(source):
        @pl.loop(0, capacity // chunk)
        def _(i):
            first = pl.multiple_of(i * chunk, chunk)
            to = pl.multiple_of(source * capacity + first, chunk)
            arrived_ref[pl.ds(to, chunk), :] = inbox_ref[source, pl.ds(first, chunk), :].astype(
                jnp.float32
            )

    widen(me)

    @pl.loop(0, count - 1)
    def _(i):
        j = lax.rem(i + count // 2, count - 1) + 1
        source = lax.rem(me - j + count, count)
        pltpu.make_async_remote_copy(
            src_ref=outbox_ref.at[source],
            dst_ref=inbox_ref.at[source],
            send_sem=send_sem.at[j],
            recv_sem=recv_sem.at[j],
            device_id={axis: source},
            device_id_type=pl.DeviceIdType.MESH,
        ).wait_recv()
        widen(source)

    @pl.loop(0, rows // chunk)
    def _(i):
        first = pl.multiple_of(i * chunk, chunk)
        for c in range(chunk):
            stage_ref[pl.ds(c, 1), :] = arrived[recv_ref[first + c]]
        out_ref[pl.ds(first, chunk), :] = stage_ref[...].astype(jnp.bfloat16)

    @pl.loop(1, count)
    def _(j):
        copy_to(j).wait_send()


def relay(blended, send_slot, recv_slot, axis):
    rows, channels = blended.shape
    count = lax.axis_size(axis)
    capacity = send_slot.shape[0] // count
    chunk = 128
    whole = pl.BlockSpec(memory_space=pltpu.VMEM)
    scalars = pl.BlockSpec(memory_space=pltpu.SMEM)
    boxes = pltpu.VMEM((count, capacity, channels), jnp.bfloat16)
    return pl.pallas_call(
        functools.partial(relay_kernel, axis=axis, count=count),
        out_shape=jax.ShapeDtypeStruct((rows, channels), jnp.bfloat16),
        in_specs=[scalars, scalars, whole],
        out_specs=whole,
        scratch_shapes=[
            pltpu.VMEM((rows + 8, channels), jnp.float32),
            pltpu.VMEM((chunk, channels), jnp.float32),
            boxes,
            boxes,
            pltpu.VMEM((count * capacity, channels), jnp.float32),
            pltpu.SemaphoreType.DMA((count,)),
            pltpu.SemaphoreType.DMA((count,)),
        ],
        compiler_params=pltpu.CompilerParams(
            collective_id=0, has_side_effects=True, vmem_limit_bytes=48 * 1024 * 1024
        ),
    )(send_slot, recv_slot, blended)


def body(
    features, neighbors, send_low, send_high, send_slot, recv_slot, kernel, norm_gain, norm_shift
):
    row_count, channels = features.shape
    weights = lax.all_gather(kernel.transpose(0, 2, 1), "grp", axis=1, tiled=True)
    upward = jnp.take(features, send_high, axis=0)
    downward = jnp.take(features, send_low, axis=0)
    from_lower = shifted(upward, "brick", 1)
    from_upper = shifted(downward, "brick", -1)
    lists, places = compact(neighbors.T, row_count + 2 * send_low.shape[0])
    blended = conv_block(
        features,
        from_lower,
        from_upper,
        lists,
        places,
        weights,
        norm_gain.reshape(1, channels),
        norm_shift.reshape(1, channels),
    )
    return relay(blended, send_slot, recv_slot, "brick")


def solution(mesh):
    return jax.shard_map(
        body,
        mesh=mesh,
        in_specs=(
            P(("brick", "grp"), None),
            P(("brick", "grp"), None),
            P(("brick", "grp")),
            P(("brick", "grp")),
            P(("brick", "grp")),
            P(("brick", "grp")),
            P(None, None, "grp"),
            P(),
            P(),
        ),
        out_specs=P(("brick", "grp"), None),
        check_vma=False,
    )
```

```python
import functools

import jax
import jax.numpy as jnp
from jax import lax
from jax.experimental import pallas as pl
from jax.experimental.pallas import tpu as pltpu
from jax.sharding import PartitionSpec as P

BLOCK = 256


def shifted(block, axis, distance):
    devices = range(lax.axis_size(axis))
    route = [(i - distance, i) for i in devices if i - distance in devices]
    return lax.ppermute(block, axis, route)


def pick_kernel(high_ref, low_ref, feat_ref, upward_ref, downward_ref, table_ref, stage_ref):
    rows, channels = feat_ref.shape
    chunk = stage_ref.shape[0]
    table = table_ref.reshape(rows, 1, channels)

    @pl.loop(0, rows // chunk)
    def _(i):
        at = pl.ds(pl.multiple_of(i * chunk, chunk), chunk)
        table_ref[at, :] = feat_ref[at, :].astype(jnp.float32)

    for index_ref, into_ref in ((high_ref, upward_ref), (low_ref, downward_ref)):

        @pl.loop(0, into_ref.shape[0] // chunk)
        def _(i, index_ref=index_ref, into_ref=into_ref):
            first = pl.multiple_of(i * chunk, chunk)
            for c in range(chunk):
                stage_ref[pl.ds(c, 1), :] = table[index_ref[first + c]]
            into_ref[pl.ds(first, chunk), :] = stage_ref[...].astype(jnp.bfloat16)


def pick_halo(features, send_high, send_low):
    rows, channels = features.shape
    halo = send_high.shape[0]
    chunk = 256
    whole = pl.BlockSpec(memory_space=pltpu.VMEM)
    scalars = pl.BlockSpec(memory_space=pltpu.SMEM)
    shape = jax.ShapeDtypeStruct((halo, channels), jnp.bfloat16)
    return pl.pallas_call(
        pick_kernel,
        out_shape=(shape, shape),
        in_specs=[scalars, scalars, whole],
        out_specs=(whole, whole),
        scratch_shapes=[
            pltpu.VMEM((rows, channels), jnp.float32),
            pltpu.VMEM((chunk, channels), jnp.float32),
        ],
        compiler_params=pltpu.CompilerParams(vmem_limit_bytes=16 * 1024 * 1024),
    )(send_high, send_low, features)


def compact_kernel(nb_ref, list_ref, pos_ref, *, absent, block):
    offsets, width = nb_ref.shape
    value = nb_ref[...]
    present = value != absent
    lane = lax.broadcasted_iota(jnp.int32, (offsets, width), 1) & (block - 1)
    before = lax.broadcasted_iota(jnp.int32, (block, block), 0)
    after = lax.broadcasted_iota(jnp.int32, (block, block), 1)
    triangle = jnp.where(before <= after, 1.0, 0.0).astype(jnp.bfloat16)
    ones = jnp.where(present, 1.0, 0.0).astype(jnp.bfloat16)
    counted = [
        jnp.dot(ones[:, at : at + block], triangle, preferred_element_type=jnp.float32)
        for at in range(0, width, block)
    ]
    pos = jnp.concatenate(counted, axis=1).astype(jnp.int32) - 1
    pos_ref[...] = jnp.where(present, pos, -1)
    word = jnp.where(present, value + (lane - pos) * 16384 + (1 << 23), 0)
    for bit in range(block.bit_length() - 1):
        moves = (word & (16384 << bit)) != 0
        moved = pltpu.roll(jnp.where(moves, word, 0), width - (1 << bit), 1)
        word = jnp.where(moves, 0, word) + moved
    list_ref[...] = jnp.where(word != 0, word & 16383, absent)


def conv_kernel(
    list_ref,
    next_ref,
    pos_ref,
    feat_ref,
    low_ref,
    up_ref,
    w_ref,
    gain_ref,
    shift_ref,
    out_ref,
    tab_ref,
    buf_a,
    buf_b,
    acc_ref,
):
    step = pl.program_id(0)
    rows, channels = feat_ref.shape
    halo = low_ref.shape[0]
    offsets, block = list_ref.shape
    half = block // 2
    middle = offsets // 2
    absent = rows + 2 * halo
    table = tab_ref.reshape(tab_ref.shape[0], 1, channels)
    slots = lax.broadcasted_iota(jnp.int32, (half, block), 0)

    @pl.when(step == 0)
    def _():
        chunk = 256
        for src, start in ((feat_ref, 0), (low_ref, rows), (up_ref, rows + halo)):

            @pl.loop(0, src.shape[0] // chunk)
            def _(i, src=src, start=start):
                at = pl.multiple_of(i * chunk, chunk)
                tab_ref[pl.ds(start + at, chunk), :] = src[pl.ds(at, chunk), :].astype(jnp.float32)

        tab_ref[pl.ds(absent, 8), :] = jnp.zeros((8, channels), jnp.float32)

    def offset_of(pair, j):
        at = 2 * pair + j
        return at + jnp.where(at >= middle, 1, 0)

    def gather(pair, buf, base=0, count=2, lists=list_ref):
        for j in range(2 * count):
            k = offset_of(pair, j)
            for c in range(half):
                buf[pl.ds(j * half + c, 1), :] = table[lists[k, base + c]]

    def multiply(pair, buf, base=0, count=2):
        total = jnp.zeros_like(acc_ref)
        for i in range(count):
            products, spreads = [], []
            for j in range(2 * i, 2 * i + 2):
                k = offset_of(pair, j)
                rows_in = buf[j * half : (j + 1) * half, :].astype(jnp.bfloat16)
                products.append(
                    lax.dot_general(
                        w_ref[k],
                        rows_in,
                        (((1,), (1,)), ((), ())),
                        preferred_element_type=jnp.float32,
                    )
                )
                wanted = pos_ref[pl.ds(k, 1), :] - base
                spreads.append(jnp.where(slots == wanted, 1.0, 0.0).astype(jnp.bfloat16))
            product = jnp.concatenate(products, axis=1)
            high = product.astype(jnp.bfloat16)
            low = (product - high.astype(jnp.float32)).astype(jnp.bfloat16)
            both = jnp.concatenate([high, low], axis=0)
            spread = jnp.concatenate(spreads, axis=0)
            result = jnp.dot(both, spread, preferred_element_type=jnp.float32)
            total += result[:channels] + result[channels:]
        acc_ref[...] += total

    own = feat_ref[pl.ds(pl.multiple_of(step * block, block), block), :]
    pairs = middle

    @pl.when(step == 0)
    def _():
        gather(0, buf_a, count=1)

    acc_ref[...] = lax.dot_general(
        w_ref[middle], own, (((1,), (1,)), ((), ())), preferred_element_type=jnp.float32
    )
    gather(1, buf_b)
    multiply(0, buf_a, count=1)

    @pl.loop(0, (pairs - 3) // 4)
    def _(p):
        first = 1 + 4 * p
        gather(first + 2, buf_a)
        multiply(first, buf_b)
        gather(first + 4, buf_b)
        multiply(first + 2, buf_a)

    gather(pairs - 2, buf_a)
    multiply(pairs - 4, buf_b)

    crowded = jnp.int32(0)
    for k in range(offsets):
        if k != middle:
            crowded = crowded + jnp.where(list_ref[k, half] != absent, 1, 0)

    @pl.when(crowded > 0)
    def _():

        @pl.loop(0, pairs)
        def _(p):
            more = (list_ref[offset_of(p, 0), half] != absent) | (
                list_ref[offset_of(p, 1), half] != absent
            )

            @pl.when(more)
            def _():
                gather(p, buf_b, half, 1)
                multiply(p, buf_b, half, 1)

    multiply(pairs - 2, buf_a)
    gather(0, buf_a, count=1, lists=next_ref)
    summed = acc_ref[...].T
    centered = summed - jnp.mean(summed, axis=-1, keepdims=True)
    spread_sq = jnp.mean(centered * centered, axis=-1, keepdims=True)
    normed = centered * lax.rsqrt(spread_sq + 1e-05) * gain_ref[...] + shift_ref[...]
    blended = own.astype(jnp.float32) + normed / (1.0 + jnp.exp(-normed))
    out_ref[...] = blended.astype(jnp.bfloat16)


def compact(columns, absent):
    offsets, rows = columns.shape
    width = 8 * BLOCK
    spec = pl.BlockSpec((offsets, width), lambda i: (0, i))
    shape = jax.ShapeDtypeStruct((offsets, rows), jnp.int32)
    return pl.pallas_call(
        functools.partial(compact_kernel, absent=absent, block=BLOCK),
        grid=(rows // width,),
        out_shape=(shape, shape),
        in_specs=[spec],
        out_specs=(spec, spec),
        cost_estimate=pl.CostEstimate(
            flops=0, bytes_accessed=200 * rows * offsets, transcendentals=0
        ),
    )(columns)


def conv_block(features, from_lower, from_upper, lists, places, weights, gain, shift):
    rows, channels = features.shape
    halo = from_lower.shape[0]
    offsets = lists.shape[0]
    block = BLOCK
    whole = pl.BlockSpec(memory_space=pltpu.VMEM)
    last = rows // block - 1
    return pl.pallas_call(
        conv_kernel,
        grid=(rows // block,),
        out_shape=jax.ShapeDtypeStruct((rows, channels), jnp.bfloat16),
        in_specs=[
            pl.BlockSpec((offsets, block), lambda i: (0, i), memory_space=pltpu.SMEM),
            pl.BlockSpec(
                (offsets, block), lambda i: (0, jnp.minimum(i + 1, last)), memory_space=pltpu.SMEM
            ),
            pl.BlockSpec((offsets, block), lambda i: (0, i)),
            whole,
            whole,
            whole,
            whole,
            whole,
            whole,
        ],
        out_specs=pl.BlockSpec((block, channels), lambda i: (i, 0)),
        scratch_shapes=[
            pltpu.VMEM((rows + 2 * halo + 8, channels), jnp.float32),
            pltpu.VMEM((2 * block, channels), jnp.float32),
            pltpu.VMEM((2 * block, channels), jnp.float32),
            pltpu.VMEM((channels, block), jnp.float32),
        ],
        compiler_params=pltpu.CompilerParams(vmem_limit_bytes=48 * 1024 * 1024),
        cost_estimate=pl.CostEstimate(
            flops=2 * rows * offsets * channels * channels,
            bytes_accessed=8 * rows * channels,
            transcendentals=rows * channels,
        ),
    )(lists, lists, places, features, from_lower, from_upper, weights, gain, shift)


def relay_kernel(
    send_ref,
    recv_ref,
    rows_ref,
    out_ref,
    table_ref,
    stage_ref,
    outbox_ref,
    inbox_ref,
    arrived_ref,
    send_sem,
    recv_sem,
    *,
    axis,
    count,
):
    me = lax.axis_index(axis)
    rows, channels = rows_ref.shape
    capacity = outbox_ref.shape[1]
    chunk = stage_ref.shape[0]
    table = table_ref.reshape(table_ref.shape[0], 1, channels)
    arrived = arrived_ref.reshape(arrived_ref.shape[0], 1, channels)

    barrier = pltpu.get_barrier_semaphore()

    @pl.loop(1, count)
    def _(j):
        pl.semaphore_signal(
            barrier,
            inc=1,
            device_id={axis: lax.rem(me + j, count)},
            device_id_type=pl.DeviceIdType.MESH,
        )

    @pl.loop(0, rows // chunk)
    def _(i):
        at = pl.ds(pl.multiple_of(i * chunk, chunk), chunk)
        table_ref[at, :] = rows_ref[at, :].astype(jnp.float32)

    table_ref[pl.ds(rows, 8), :] = jnp.zeros((8, channels), jnp.float32)
    pl.semaphore_wait(barrier, count - 1)

    def copy_to(j):
        to = lax.rem(me + j, count)
        return pltpu.make_async_remote_copy(
            src_ref=outbox_ref.at[to],
            dst_ref=inbox_ref.at[me],
            send_sem=send_sem.at[j],
            recv_sem=recv_sem.at[j],
            device_id={axis: to},
            device_id_type=pl.DeviceIdType.MESH,
        )

    def fill(shard, into_ref):
        @pl.loop(0, capacity // chunk)
        def _(i):
            first = pl.multiple_of(i * chunk, chunk)
            for c in range(chunk):
                stage_ref[pl.ds(c, 1), :] = table[send_ref[shard * capacity + first + c]]
            into_ref[pl.ds(first, chunk), :] = stage_ref[...].astype(jnp.bfloat16)

    @pl.loop(0, count - 1)
    def _(i):
        j = lax.rem(i + count // 2, count - 1) + 1
        fill(lax.rem(me + j, count), outbox_ref.at[lax.rem(me + j, count)])
        copy_to(j).start()

    fill(me, inbox_ref.at[me])

    def widen(source):
        @pl.loop(0, capacity // chunk)
        def _(i):
            first = pl.multiple_of(i * chunk, chunk)
            to = pl.multiple_of(source * capacity + first, chunk)
            arrived_ref[pl.ds(to, chunk), :] = inbox_ref[source, pl.ds(first, chunk), :].astype(
                jnp.float32
            )

    widen(me)

    @pl.loop(0, count - 1)
    def _(i):
        j = lax.rem(i + count // 2, count - 1) + 1
        source = lax.rem(me - j + count, count)
        pltpu.make_async_remote_copy(
            src_ref=outbox_ref.at[source],
            dst_ref=inbox_ref.at[source],
            send_sem=send_sem.at[j],
            recv_sem=recv_sem.at[j],
            device_id={axis: source},
            device_id_type=pl.DeviceIdType.MESH,
        ).wait_recv()
        widen(source)

    @pl.loop(0, rows // chunk)
    def _(i):
        first = pl.multiple_of(i * chunk, chunk)
        for c in range(chunk):
            stage_ref[pl.ds(c, 1), :] = arrived[recv_ref[first + c]]
        out_ref[pl.ds(first, chunk), :] = stage_ref[...].astype(jnp.bfloat16)

    @pl.loop(1, count)
    def _(j):
        copy_to(j).wait_send()


def relay(blended, send_slot, recv_slot, axis):
    rows, channels = blended.shape
    count = lax.axis_size(axis)
    capacity = send_slot.shape[0] // count
    chunk = 128
    whole = pl.BlockSpec(memory_space=pltpu.VMEM)
    scalars = pl.BlockSpec(memory_space=pltpu.SMEM)
    boxes = pltpu.VMEM((count, capacity, channels), jnp.bfloat16)
    return pl.pallas_call(
        functools.partial(relay_kernel, axis=axis, count=count),
        out_shape=jax.ShapeDtypeStruct((rows, channels), jnp.bfloat16),
        in_specs=[scalars, scalars, whole],
        out_specs=whole,
        scratch_shapes=[
            pltpu.VMEM((rows + 8, channels), jnp.float32),
            pltpu.VMEM((chunk, channels), jnp.float32),
            boxes,
            boxes,
            pltpu.VMEM((count * capacity, channels), jnp.float32),
            pltpu.SemaphoreType.DMA((count,)),
            pltpu.SemaphoreType.DMA((count,)),
        ],
        compiler_params=pltpu.CompilerParams(
            collective_id=0, has_side_effects=True, vmem_limit_bytes=48 * 1024 * 1024
        ),
    )(send_slot, recv_slot, blended)


def body(
    features, neighbors, send_low, send_high, send_slot, recv_slot, kernel, norm_gain, norm_shift
):
    row_count, channels = features.shape
    weights = lax.all_gather(kernel.transpose(0, 2, 1), "grp", axis=1, tiled=True)
    upward, downward = pick_halo(features, send_high, send_low)
    from_lower = shifted(upward, "brick", 1)
    from_upper = shifted(downward, "brick", -1)
    lists, places = compact(neighbors.T, row_count + 2 * send_low.shape[0])
    blended = conv_block(
        features,
        from_lower,
        from_upper,
        lists,
        places,
        weights,
        norm_gain.reshape(1, channels),
        norm_shift.reshape(1, channels),
    )
    return relay(blended, send_slot, recv_slot, "brick")


def solution(mesh):
    return jax.shard_map(
        body,
        mesh=mesh,
        in_specs=(
            P(("brick", "grp"), None),
            P(("brick", "grp"), None),
            P(("brick", "grp")),
            P(("brick", "grp")),
            P(("brick", "grp")),
            P(("brick", "grp")),
            P(None, None, "grp"),
            P(),
            P(),
        ),
        out_specs=P(("brick", "grp"), None),
        check_vma=False,
    )
```

```python
import functools

import jax
import jax.numpy as jnp
from jax import lax
from jax.experimental import pallas as pl
from jax.experimental.pallas import tpu as pltpu
from jax.sharding import PartitionSpec as P

BLOCK = 256


def shifted(block, axis, distance):
    devices = range(lax.axis_size(axis))
    route = [(i - distance, i) for i in devices if i - distance in devices]
    return lax.ppermute(block, axis, route)


def pick_kernel(high_ref, low_ref, feat_ref, upward_ref, downward_ref, table_ref, stage_ref):
    rows, channels = feat_ref.shape
    chunk = stage_ref.shape[0]
    table = table_ref.reshape(rows, 1, channels)

    @pl.loop(0, rows // chunk)
    def _(i):
        at = pl.ds(pl.multiple_of(i * chunk, chunk), chunk)
        table_ref[at, :] = feat_ref[at, :].astype(jnp.float32)

    for index_ref, into_ref in ((high_ref, upward_ref), (low_ref, downward_ref)):

        @pl.loop(0, into_ref.shape[0] // chunk)
        def _(i, index_ref=index_ref, into_ref=into_ref):
            first = pl.multiple_of(i * chunk, chunk)
            for c in range(chunk):
                stage_ref[pl.ds(c, 1), :] = table[index_ref[first + c]]
            into_ref[pl.ds(first, chunk), :] = stage_ref[...].astype(jnp.bfloat16)


def pick_halo(features, send_high, send_low):
    rows, channels = features.shape
    halo = send_high.shape[0]
    chunk = 256
    whole = pl.BlockSpec(memory_space=pltpu.VMEM)
    scalars = pl.BlockSpec(memory_space=pltpu.SMEM)
    shape = jax.ShapeDtypeStruct((halo, channels), jnp.bfloat16)
    return pl.pallas_call(
        pick_kernel,
        out_shape=(shape, shape),
        in_specs=[scalars, scalars, whole],
        out_specs=(whole, whole),
        scratch_shapes=[
            pltpu.VMEM((rows, channels), jnp.float32),
            pltpu.VMEM((chunk, channels), jnp.float32),
        ],
        compiler_params=pltpu.CompilerParams(vmem_limit_bytes=16 * 1024 * 1024),
    )(send_high, send_low, features)


def compact_kernel(nb_ref, list_ref, pos_ref, *, absent, block):
    offsets, width = nb_ref.shape
    value = nb_ref[...]
    present = value != absent
    lane = lax.broadcasted_iota(jnp.int32, (offsets, width), 1) & (block - 1)
    before = lax.broadcasted_iota(jnp.int32, (block, block), 0)
    after = lax.broadcasted_iota(jnp.int32, (block, block), 1)
    triangle = jnp.where(before <= after, 1.0, 0.0).astype(jnp.bfloat16)
    ones = jnp.where(present, 1.0, 0.0).astype(jnp.bfloat16)
    counted = [
        jnp.dot(ones[:, at : at + block], triangle, preferred_element_type=jnp.float32)
        for at in range(0, width, block)
    ]
    pos = jnp.concatenate(counted, axis=1).astype(jnp.int32) - 1
    pos_ref[...] = jnp.where(present, pos, -1)
    word = jnp.where(present, value + (lane - pos) * 16384 + (1 << 23), 0)
    for bit in range(block.bit_length() - 1):
        moves = (word & (16384 << bit)) != 0
        moved = pltpu.roll(jnp.where(moves, word, 0), width - (1 << bit), 1)
        word = jnp.where(moves, 0, word) + moved
    list_ref[...] = jnp.where(word != 0, word & 16383, absent)


def conv_kernel(
    list_ref,
    next_ref,
    pos_ref,
    feat_ref,
    low_ref,
    up_ref,
    place_ref,
    mine_ref,
    got_ref,
    passed_ref,
    gain_ref,
    shift_ref,
    out_ref,
    w_ref,
    tab_ref,
    buf_a,
    buf_b,
    acc_ref,
):
    step = pl.program_id(0)
    rows, channels = feat_ref.shape
    halo = low_ref.shape[0]
    offsets, block = list_ref.shape
    half = block // 2
    middle = offsets // 2
    absent = rows + 2 * halo
    table = tab_ref.reshape(tab_ref.shape[0], 1, channels)
    slots = lax.broadcasted_iota(jnp.int32, (half, block), 0)
    slots = slots.astype(jnp.float32).astype(jnp.bfloat16)
    one, zero = jnp.bfloat16(1), jnp.bfloat16(0)

    @pl.when(step == 0)
    def _():
        chunk = 256
        for src, start in ((feat_ref, 0), (low_ref, rows), (up_ref, rows + halo)):

            @pl.loop(0, src.shape[0] // chunk)
            def _(i, src=src, start=start):
                at = pl.multiple_of(i * chunk, chunk)
                tab_ref[pl.ds(start + at, chunk), :] = src[pl.ds(at, chunk), :].astype(jnp.float32)

        tab_ref[pl.ds(absent, 8), :] = jnp.zeros((8, channels), jnp.float32)

        columns = mine_ref.shape[1]
        part = columns // 2
        groups = got_ref.shape[0] + 1
        group, core = place_ref[0], place_ref[1]
        at = pl.multiple_of(group * columns, columns)
        w_ref[:, pl.ds(at, columns), :] = mine_ref[...]
        for j in range(groups - 1):
            source = lax.rem(group - j - 1 + groups, groups)
            for ref, which in ((got_ref, core), (passed_ref, 1 - core)):
                at = pl.multiple_of(source * columns + which * part, part)
                w_ref[:, pl.ds(at, part), :] = ref[j]

    def offset_of(pair, j):
        at = 2 * pair + j
        return at + jnp.where(at >= middle, 1, 0)

    def gather(pair, buf, base=0, count=2, lists=list_ref):
        for j in range(2 * count):
            k = offset_of(pair, j)
            for c in range(half):
                buf[pl.ds(j * half + c, 1), :] = table[lists[k, base + c]]

    def multiply(pair, buf, base=0, count=2):
        products, spreads = [], []
        for j in range(2 * count):
            k = offset_of(pair, j)
            rows_in = buf[j * half : (j + 1) * half, :].astype(jnp.bfloat16)
            products.append(
                lax.dot_general(
                    w_ref[k], rows_in, (((1,), (1,)), ((), ())), preferred_element_type=jnp.float32
                )
            )
            wanted = (pos_ref[pl.ds(k, 1), :] - base).astype(jnp.float32).astype(jnp.bfloat16)
            spreads.append(jnp.where(slots == wanted, one, zero))
        product = jnp.concatenate(products, axis=1)
        high = product.astype(jnp.bfloat16)
        low = (product - high.astype(jnp.float32)).astype(jnp.bfloat16)
        both = jnp.concatenate([high, low], axis=0)
        spread = jnp.concatenate(spreads, axis=0)
        result = jnp.dot(both, spread, preferred_element_type=jnp.float32)
        acc_ref[...] += result[:channels] + result[channels:]

    own = feat_ref[pl.ds(pl.multiple_of(step * block, block), block), :]
    pairs = middle

    @pl.when(step == 0)
    def _():
        gather(0, buf_a, count=1)

    acc_ref[...] = lax.dot_general(
        w_ref[middle], own, (((1,), (1,)), ((), ())), preferred_element_type=jnp.float32
    )
    gather(1, buf_b)
    multiply(0, buf_a, count=1)

    @pl.loop(0, (pairs - 3) // 4)
    def _(p):
        first = 1 + 4 * p
        gather(first + 2, buf_a)
        multiply(first, buf_b)
        gather(first + 4, buf_b)
        multiply(first + 2, buf_a)

    gather(pairs - 2, buf_a)
    multiply(pairs - 4, buf_b)

    crowded = jnp.int32(0)
    for k in range(offsets):
        if k != middle:
            crowded = crowded + jnp.where(list_ref[k, half] != absent, 1, 0)

    @pl.when(crowded > 0)
    def _():

        @pl.loop(0, pairs)
        def _(p):
            more = (list_ref[offset_of(p, 0), half] != absent) | (
                list_ref[offset_of(p, 1), half] != absent
            )

            @pl.when(more)
            def _():
                gather(p, buf_b, half, 1)
                multiply(p, buf_b, half, 1)

    multiply(pairs - 2, buf_a)
    gather(0, buf_a, count=1, lists=next_ref)
    summed = acc_ref[...].T
    centered = summed - jnp.mean(summed, axis=-1, keepdims=True)
    spread_sq = jnp.mean(centered * centered, axis=-1, keepdims=True)
    normed = centered * lax.rsqrt(spread_sq + 1e-05) * gain_ref[...] + shift_ref[...]
    blended = own.astype(jnp.float32) + normed / (1.0 + jnp.exp(-normed))
    out_ref[...] = blended.astype(jnp.bfloat16)


def compact(columns, absent):
    offsets, rows = columns.shape
    width = 8 * BLOCK
    spec = pl.BlockSpec((offsets, width), lambda i: (0, i))
    shape = jax.ShapeDtypeStruct((offsets, rows), jnp.int32)
    return pl.pallas_call(
        functools.partial(compact_kernel, absent=absent, block=BLOCK),
        grid=(rows // width,),
        out_shape=(shape, shape),
        in_specs=[spec],
        out_specs=(spec, spec),
        cost_estimate=pl.CostEstimate(
            flops=0, bytes_accessed=200 * rows * offsets, transcendentals=0
        ),
    )(columns)


def conv_block(features, from_lower, from_upper, lists, places, weights, gain, shift):
    place, mine, got, passed = weights
    rows, channels = features.shape
    halo = from_lower.shape[0]
    offsets = lists.shape[0]
    block = BLOCK
    whole = pl.BlockSpec(memory_space=pltpu.VMEM)
    last = rows // block - 1
    return pl.pallas_call(
        conv_kernel,
        grid=(rows // block,),
        out_shape=jax.ShapeDtypeStruct((rows, channels), jnp.bfloat16),
        in_specs=[
            pl.BlockSpec((offsets, block), lambda i: (0, i), memory_space=pltpu.SMEM),
            pl.BlockSpec(
                (offsets, block), lambda i: (0, jnp.minimum(i + 1, last)), memory_space=pltpu.SMEM
            ),
            pl.BlockSpec((offsets, block), lambda i: (0, i)),
            whole,
            whole,
            whole,
            pl.BlockSpec(memory_space=pltpu.SMEM),
            whole,
            whole,
            whole,
            whole,
            whole,
        ],
        out_specs=pl.BlockSpec((block, channels), lambda i: (i, 0)),
        scratch_shapes=[
            pltpu.VMEM((offsets, channels, channels), jnp.bfloat16),
            pltpu.VMEM((rows + 2 * halo + 8, channels), jnp.float32),
            pltpu.VMEM((2 * block, channels), jnp.float32),
            pltpu.VMEM((2 * block, channels), jnp.float32),
            pltpu.VMEM((channels, block), jnp.float32),
        ],
        compiler_params=pltpu.CompilerParams(vmem_limit_bytes=48 * 1024 * 1024),
        cost_estimate=pl.CostEstimate(
            flops=2 * rows * offsets * channels * channels,
            bytes_accessed=8 * rows * channels,
            transcendentals=rows * channels,
        ),
    )(
        lists,
        lists,
        places,
        features,
        from_lower,
        from_upper,
        place,
        mine,
        got,
        passed,
        gain,
        shift,
    )


def relay_kernel(
    send_ref,
    recv_ref,
    rows_ref,
    out_ref,
    table_ref,
    stage_ref,
    outbox_ref,
    inbox_ref,
    arrived_ref,
    send_sem,
    recv_sem,
    *,
    axis,
    count,
):
    me = lax.axis_index(axis)
    rows, channels = rows_ref.shape
    capacity = outbox_ref.shape[1]
    chunk = stage_ref.shape[0]
    table = table_ref.reshape(table_ref.shape[0], 1, channels)
    arrived = arrived_ref.reshape(arrived_ref.shape[0], 1, channels)

    barrier = pltpu.get_barrier_semaphore()

    @pl.loop(1, count)
    def _(j):
        pl.semaphore_signal(
            barrier,
            inc=1,
            device_id={axis: lax.rem(me + j, count)},
            device_id_type=pl.DeviceIdType.MESH,
        )

    @pl.loop(0, rows // chunk)
    def _(i):
        at = pl.ds(pl.multiple_of(i * chunk, chunk), chunk)
        table_ref[at, :] = rows_ref[at, :].astype(jnp.float32)

    table_ref[pl.ds(rows, 8), :] = jnp.zeros((8, channels), jnp.float32)
    pl.semaphore_wait(barrier, count - 1)

    def copy_to(j):
        to = lax.rem(me + j, count)
        return pltpu.make_async_remote_copy(
            src_ref=outbox_ref.at[to],
            dst_ref=inbox_ref.at[me],
            send_sem=send_sem.at[j],
            recv_sem=recv_sem.at[j],
            device_id={axis: to},
            device_id_type=pl.DeviceIdType.MESH,
        )

    def fill(shard, into_ref):
        @pl.loop(0, capacity // chunk)
        def _(i):
            first = pl.multiple_of(i * chunk, chunk)
            for c in range(chunk):
                stage_ref[pl.ds(c, 1), :] = table[send_ref[shard * capacity + first + c]]
            into_ref[pl.ds(first, chunk), :] = stage_ref[...].astype(jnp.bfloat16)

    @pl.loop(0, count - 1)
    def _(i):
        j = lax.rem(i + count // 2, count - 1) + 1
        fill(lax.rem(me + j, count), outbox_ref.at[lax.rem(me + j, count)])
        copy_to(j).start()

    fill(me, inbox_ref.at[me])

    def widen(source):
        @pl.loop(0, capacity // chunk)
        def _(i):
            first = pl.multiple_of(i * chunk, chunk)
            to = pl.multiple_of(source * capacity + first, chunk)
            arrived_ref[pl.ds(to, chunk), :] = inbox_ref[source, pl.ds(first, chunk), :].astype(
                jnp.float32
            )

    widen(me)

    @pl.loop(0, count - 1)
    def _(i):
        j = lax.rem(i + count // 2, count - 1) + 1
        source = lax.rem(me - j + count, count)
        pltpu.make_async_remote_copy(
            src_ref=outbox_ref.at[source],
            dst_ref=inbox_ref.at[source],
            send_sem=send_sem.at[j],
            recv_sem=recv_sem.at[j],
            device_id={axis: source},
            device_id_type=pl.DeviceIdType.MESH,
        ).wait_recv()
        widen(source)

    @pl.loop(0, rows // chunk)
    def _(i):
        first = pl.multiple_of(i * chunk, chunk)
        for c in range(chunk):
            stage_ref[pl.ds(c, 1), :] = arrived[recv_ref[first + c]]
        out_ref[pl.ds(first, chunk), :] = stage_ref[...].astype(jnp.bfloat16)

    @pl.loop(1, count)
    def _(j):
        copy_to(j).wait_send()


def relay(blended, send_slot, recv_slot, axis):
    rows, channels = blended.shape
    count = lax.axis_size(axis)
    capacity = send_slot.shape[0] // count
    chunk = 128
    whole = pl.BlockSpec(memory_space=pltpu.VMEM)
    scalars = pl.BlockSpec(memory_space=pltpu.SMEM)
    boxes = pltpu.VMEM((count, capacity, channels), jnp.bfloat16)
    return pl.pallas_call(
        functools.partial(relay_kernel, axis=axis, count=count),
        out_shape=jax.ShapeDtypeStruct((rows, channels), jnp.bfloat16),
        in_specs=[scalars, scalars, whole],
        out_specs=whole,
        scratch_shapes=[
            pltpu.VMEM((rows + 8, channels), jnp.float32),
            pltpu.VMEM((chunk, channels), jnp.float32),
            boxes,
            boxes,
            pltpu.VMEM((count * capacity, channels), jnp.float32),
            pltpu.SemaphoreType.DMA((count,)),
            pltpu.SemaphoreType.DMA((count,)),
        ],
        compiler_params=pltpu.CompilerParams(
            collective_id=0, has_side_effects=True, vmem_limit_bytes=48 * 1024 * 1024
        ),
    )(send_slot, recv_slot, blended)


def spread_weights(mine):
    slabs, groups = lax.axis_size("brick"), lax.axis_size("grp")
    core = lax.rem(lax.axis_index("brick"), 2)
    part = mine.shape[1] // 2
    half = lax.dynamic_slice_in_dim(mine, core * part, part, axis=1)
    got = [
        lax.ppermute(half, "grp", [(i, (i + j) % groups) for i in range(groups)])
        for j in range(1, groups)
    ]
    got = jnp.stack(got)
    passed = lax.ppermute(got, "brick", [(i, i ^ 1) for i in range(slabs)])
    place = jnp.stack([lax.axis_index("grp"), core]).astype(jnp.int32)
    return place, mine, got, passed


def body(
    features, neighbors, send_low, send_high, send_slot, recv_slot, kernel, norm_gain, norm_shift
):
    row_count, channels = features.shape
    weights = spread_weights(kernel.transpose(0, 2, 1))
    upward, downward = pick_halo(features, send_high, send_low)
    from_lower = shifted(upward, "brick", 1)
    from_upper = shifted(downward, "brick", -1)
    lists, places = compact(neighbors.T, row_count + 2 * send_low.shape[0])
    blended = conv_block(
        features,
        from_lower,
        from_upper,
        lists,
        places,
        weights,
        norm_gain.reshape(1, channels),
        norm_shift.reshape(1, channels),
    )
    return relay(blended, send_slot, recv_slot, "brick")


def solution(mesh):
    return jax.shard_map(
        body,
        mesh=mesh,
        in_specs=(
            P(("brick", "grp"), None),
            P(("brick", "grp"), None),
            P(("brick", "grp")),
            P(("brick", "grp")),
            P(("brick", "grp")),
            P(("brick", "grp")),
            P(None, None, "grp"),
            P(),
            P(),
        ),
        out_specs=P(("brick", "grp"), None),
        check_vma=False,
    )
```

```python
import functools

import jax
import jax.numpy as jnp
from jax import lax
from jax.experimental import pallas as pl
from jax.experimental.pallas import tpu as pltpu
from jax.sharding import PartitionSpec as P

BLOCK = 256


def shifted(block, axis, distance):
    devices = range(lax.axis_size(axis))
    route = [(i - distance, i) for i in devices if i - distance in devices]
    return lax.ppermute(block, axis, route)


def pick_kernel(high_ref, low_ref, feat_ref, upward_ref, downward_ref, table_ref, stage_ref):
    rows, channels = feat_ref.shape
    chunk = stage_ref.shape[0]
    table = table_ref.reshape(rows, 1, channels)

    @pl.loop(0, rows // chunk)
    def _(i):
        at = pl.ds(pl.multiple_of(i * chunk, chunk), chunk)
        table_ref[at, :] = feat_ref[at, :].astype(jnp.float32)

    for index_ref, into_ref in ((high_ref, upward_ref), (low_ref, downward_ref)):

        @pl.loop(0, into_ref.shape[0] // chunk)
        def _(i, index_ref=index_ref, into_ref=into_ref):
            first = pl.multiple_of(i * chunk, chunk)
            for c in range(chunk):
                stage_ref[pl.ds(c, 1), :] = table[index_ref[first + c]]
            into_ref[pl.ds(first, chunk), :] = stage_ref[...].astype(jnp.bfloat16)


def pick_halo(features, send_high, send_low):
    rows, channels = features.shape
    halo = send_high.shape[0]
    chunk = 256
    whole = pl.BlockSpec(memory_space=pltpu.VMEM)
    scalars = pl.BlockSpec(memory_space=pltpu.SMEM)
    shape = jax.ShapeDtypeStruct((halo, channels), jnp.bfloat16)
    return pl.pallas_call(
        pick_kernel,
        out_shape=(shape, shape),
        in_specs=[scalars, scalars, whole],
        out_specs=(whole, whole),
        scratch_shapes=[
            pltpu.VMEM((rows, channels), jnp.float32),
            pltpu.VMEM((chunk, channels), jnp.float32),
        ],
        compiler_params=pltpu.CompilerParams(vmem_limit_bytes=16 * 1024 * 1024),
    )(send_high, send_low, features)


def compact_kernel(nb_ref, list_ref, pos_ref, *, absent, block):
    offsets, width = nb_ref.shape
    value = nb_ref[...]
    present = value != absent
    lane = lax.broadcasted_iota(jnp.int32, (offsets, width), 1) & (block - 1)
    before = lax.broadcasted_iota(jnp.int32, (block, block), 0)
    after = lax.broadcasted_iota(jnp.int32, (block, block), 1)
    triangle = jnp.where(before <= after, 1.0, 0.0).astype(jnp.bfloat16)
    ones = jnp.where(present, 1.0, 0.0).astype(jnp.bfloat16)
    counted = [
        jnp.dot(ones[:, at : at + block], triangle, preferred_element_type=jnp.float32)
        for at in range(0, width, block)
    ]
    pos = jnp.concatenate(counted, axis=1).astype(jnp.int32) - 1
    pos_ref[...] = jnp.where(present, pos, -1)
    word = jnp.where(present, value + (lane - pos) * 16384 + (1 << 23), 0)
    for bit in range(block.bit_length() - 1):
        moves = (word & (16384 << bit)) != 0
        moved = pltpu.roll(jnp.where(moves, word, 0), width - (1 << bit), 1)
        word = jnp.where(moves, 0, word) + moved
    list_ref[...] = jnp.where(word != 0, word & 16383, absent)


def conv_kernel(
    list_ref,
    next_ref,
    pos_ref,
    feat_ref,
    low_ref,
    up_ref,
    place_ref,
    mine_ref,
    got_ref,
    passed_ref,
    gain_ref,
    shift_ref,
    out_ref,
    w_ref,
    tab_ref,
    buf_a,
    buf_b,
    buf_c,
    acc_ref,
    done_ref,
):
    step = pl.program_id(0)
    steps = pl.num_programs(0) - 1
    rows, channels = feat_ref.shape
    halo = low_ref.shape[0]
    offsets, block = list_ref.shape
    half = block // 2
    middle = offsets // 2
    absent = rows + 2 * halo
    table = tab_ref.reshape(tab_ref.shape[0], 1, channels)
    slots = lax.broadcasted_iota(jnp.int32, (half, block), 0)
    slots = slots.astype(jnp.float32).astype(jnp.bfloat16)
    one, zero = jnp.bfloat16(1), jnp.bfloat16(0)

    @pl.when(step == 0)
    def _():
        chunk = 256
        for src, start in ((feat_ref, 0), (low_ref, rows), (up_ref, rows + halo)):

            @pl.loop(0, src.shape[0] // chunk)
            def _(i, src=src, start=start):
                at = pl.multiple_of(i * chunk, chunk)
                tab_ref[pl.ds(start + at, chunk), :] = src[pl.ds(at, chunk), :].astype(jnp.float32)

        tab_ref[pl.ds(absent, 8), :] = jnp.zeros((8, channels), jnp.float32)

        columns = mine_ref.shape[1]
        part = columns // 2
        groups = got_ref.shape[0] + 1
        group, core = place_ref[0], place_ref[1]
        at = pl.multiple_of(group * columns, columns)
        w_ref[:, pl.ds(at, columns), :] = mine_ref[...]
        for j in range(groups - 1):
            source = lax.rem(group - j - 1 + groups, groups)
            for ref, which in ((got_ref, core), (passed_ref, 1 - core)):
                at = pl.multiple_of(source * columns + which * part, part)
                w_ref[:, pl.ds(at, part), :] = ref[j]

    def offset_of(pair, j):
        at = 2 * pair + j
        return at + jnp.where(at >= middle, 1, 0)

    def gather(pair, buf, base=0, count=2, lists=list_ref):
        for j in range(2 * count):
            k = offset_of(pair, j)
            for c in range(half):
                buf[pl.ds(j * half + c, 1), :] = table[lists[k, base + c]]

    def multiply(pair, buf, base=0, count=2):
        products, spreads = [], []
        for j in range(2 * count):
            k = offset_of(pair, j)
            rows_in = buf[j * half : (j + 1) * half, :].astype(jnp.bfloat16)
            products.append(
                lax.dot_general(
                    w_ref[k], rows_in, (((1,), (1,)), ((), ())), preferred_element_type=jnp.float32
                )
            )
            wanted = (pos_ref[pl.ds(k, 1), :] - base).astype(jnp.float32).astype(jnp.bfloat16)
            spreads.append(jnp.where(slots == wanted, one, zero))
        product = jnp.concatenate(products, axis=1)
        high = product.astype(jnp.bfloat16)
        low = (product - high.astype(jnp.float32)).astype(jnp.bfloat16)
        both = jnp.concatenate([high, low], axis=0)
        spread = jnp.concatenate(spreads, axis=0)
        result = jnp.dot(both, spread, preferred_element_type=jnp.float32)
        acc_ref[...] += result[:channels] + result[channels:]

    def own_rows(at):
        return feat_ref[pl.ds(pl.multiple_of(at * block, block), block), :]

    def finish(at):
        summed = done_ref[...]
        centered = summed - jnp.mean(summed, axis=0, keepdims=True)
        spread_sq = jnp.mean(centered * centered, axis=0, keepdims=True)
        normed = centered * lax.rsqrt(spread_sq + 1e-05) * gain_ref[...] + shift_ref[...]
        active = normed / (1.0 + jnp.exp(-normed))
        blended = own_rows(at).astype(jnp.float32) + active.T
        out_ref[...] = blended.astype(jnp.bfloat16)

    pairs = middle

    @pl.when(step == 0)
    def _():
        gather(0, buf_a)

    @pl.when(step < steps)
    def _():
        gather(2, buf_b)
        finish(jnp.maximum(step - 1, 0))
        acc_ref[...] = lax.dot_general(
            w_ref[middle],
            own_rows(step),
            (((1,), (1,)), ((), ())),
            preferred_element_type=jnp.float32,
        )
        multiply(0, buf_a)

        @pl.loop(0, (pairs - 5) // 4)
        def _(p):
            first = 4 * p + 2
            gather(first + 2, buf_a)
            multiply(first, buf_b)
            gather(first + 4, buf_b)
            multiply(first + 2, buf_a)

        gather(pairs - 1, buf_c, count=1)
        multiply(pairs - 3, buf_b)

        crowded = jnp.int32(0)
        for k in range(offsets):
            if k != middle:
                crowded = crowded + jnp.where(list_ref[k, half] != absent, 1, 0)

        @pl.when(crowded > 0)
        def _():

            @pl.loop(0, pairs)
            def _(p):
                more = (list_ref[offset_of(p, 0), half] != absent) | (
                    list_ref[offset_of(p, 1), half] != absent
                )

                @pl.when(more)
                def _():
                    gather(p, buf_b, half, 1)
                    multiply(p, buf_b, half, 1)

        gather(0, buf_a, lists=next_ref)
        multiply(pairs - 1, buf_c, count=1)
        done_ref[...] = acc_ref[...]

    @pl.when(step == steps)
    def _():
        finish(steps - 1)


def compact(columns, absent):
    offsets, rows = columns.shape
    width = 8 * BLOCK
    spec = pl.BlockSpec((offsets, width), lambda i: (0, i))
    shape = jax.ShapeDtypeStruct((offsets, rows), jnp.int32)
    return pl.pallas_call(
        functools.partial(compact_kernel, absent=absent, block=BLOCK),
        grid=(rows // width,),
        out_shape=(shape, shape),
        in_specs=[spec],
        out_specs=(spec, spec),
        cost_estimate=pl.CostEstimate(
            flops=0, bytes_accessed=200 * rows * offsets, transcendentals=0
        ),
    )(columns)


def conv_block(features, from_lower, from_upper, lists, places, weights, gain, shift):
    place, mine, got, passed = weights
    rows, channels = features.shape
    halo = from_lower.shape[0]
    offsets = lists.shape[0]
    block = BLOCK
    whole = pl.BlockSpec(memory_space=pltpu.VMEM)
    last = rows // block - 1
    return pl.pallas_call(
        conv_kernel,
        grid=(rows // block + 1,),
        out_shape=jax.ShapeDtypeStruct((rows, channels), jnp.bfloat16),
        in_specs=[
            pl.BlockSpec(
                (offsets, block), lambda i: (0, jnp.minimum(i, last)), memory_space=pltpu.SMEM
            ),
            pl.BlockSpec(
                (offsets, block), lambda i: (0, jnp.minimum(i + 1, last)), memory_space=pltpu.SMEM
            ),
            pl.BlockSpec((offsets, block), lambda i: (0, jnp.minimum(i, last))),
            whole,
            whole,
            whole,
            pl.BlockSpec(memory_space=pltpu.SMEM),
            whole,
            whole,
            whole,
            whole,
            whole,
        ],
        out_specs=pl.BlockSpec((block, channels), lambda i: (jnp.maximum(i - 1, 0), 0)),
        scratch_shapes=[
            pltpu.VMEM((offsets, channels, channels), jnp.bfloat16),
            pltpu.VMEM((rows + 2 * halo + 8, channels), jnp.float32),
            pltpu.VMEM((2 * block, channels), jnp.float32),
            pltpu.VMEM((2 * block, channels), jnp.float32),
            pltpu.VMEM((block, channels), jnp.float32),
            pltpu.VMEM((channels, block), jnp.float32),
            pltpu.VMEM((channels, block), jnp.float32),
        ],
        compiler_params=pltpu.CompilerParams(vmem_limit_bytes=48 * 1024 * 1024),
        cost_estimate=pl.CostEstimate(
            flops=2 * rows * offsets * channels * channels,
            bytes_accessed=8 * rows * channels,
            transcendentals=rows * channels,
        ),
    )(
        lists,
        lists,
        places,
        features,
        from_lower,
        from_upper,
        place,
        mine,
        got,
        passed,
        gain,
        shift,
    )


def relay_kernel(
    send_ref,
    recv_ref,
    rows_ref,
    out_ref,
    table_ref,
    stage_ref,
    outbox_ref,
    inbox_ref,
    arrived_ref,
    send_sem,
    recv_sem,
    *,
    axis,
    count,
):
    me = lax.axis_index(axis)
    rows, channels = rows_ref.shape
    capacity = outbox_ref.shape[1]
    chunk = stage_ref.shape[0]
    table = table_ref.reshape(table_ref.shape[0], 1, channels)
    arrived = arrived_ref.reshape(arrived_ref.shape[0], 1, channels)

    barrier = pltpu.get_barrier_semaphore()

    @pl.loop(1, count)
    def _(j):
        pl.semaphore_signal(
            barrier,
            inc=1,
            device_id={axis: lax.rem(me + j, count)},
            device_id_type=pl.DeviceIdType.MESH,
        )

    @pl.loop(0, rows // chunk)
    def _(i):
        at = pl.ds(pl.multiple_of(i * chunk, chunk), chunk)
        table_ref[at, :] = rows_ref[at, :].astype(jnp.float32)

    table_ref[pl.ds(rows, 8), :] = jnp.zeros((8, channels), jnp.float32)
    pl.semaphore_wait(barrier, count - 1)

    def copy_to(j):
        to = lax.rem(me + j, count)
        return pltpu.make_async_remote_copy(
            src_ref=outbox_ref.at[to],
            dst_ref=inbox_ref.at[me],
            send_sem=send_sem.at[j],
            recv_sem=recv_sem.at[j],
            device_id={axis: to},
            device_id_type=pl.DeviceIdType.MESH,
        )

    def fill(shard, into_ref):
        @pl.loop(0, capacity // chunk)
        def _(i):
            first = pl.multiple_of(i * chunk, chunk)
            for c in range(chunk):
                stage_ref[pl.ds(c, 1), :] = table[send_ref[shard * capacity + first + c]]
            into_ref[pl.ds(first, chunk), :] = stage_ref[...].astype(jnp.bfloat16)

    @pl.loop(0, count - 1)
    def _(i):
        j = lax.rem(i + count // 2, count - 1) + 1
        fill(lax.rem(me + j, count), outbox_ref.at[lax.rem(me + j, count)])
        copy_to(j).start()

    fill(me, inbox_ref.at[me])

    def widen(source):
        @pl.loop(0, capacity // chunk)
        def _(i):
            first = pl.multiple_of(i * chunk, chunk)
            to = pl.multiple_of(source * capacity + first, chunk)
            arrived_ref[pl.ds(to, chunk), :] = inbox_ref[source, pl.ds(first, chunk), :].astype(
                jnp.float32
            )

    widen(me)

    @pl.loop(0, count - 1)
    def _(i):
        j = lax.rem(i + count // 2, count - 1) + 1
        source = lax.rem(me - j + count, count)
        pltpu.make_async_remote_copy(
            src_ref=outbox_ref.at[source],
            dst_ref=inbox_ref.at[source],
            send_sem=send_sem.at[j],
            recv_sem=recv_sem.at[j],
            device_id={axis: source},
            device_id_type=pl.DeviceIdType.MESH,
        ).wait_recv()
        widen(source)

    @pl.loop(0, rows // chunk)
    def _(i):
        first = pl.multiple_of(i * chunk, chunk)
        for c in range(chunk):
            stage_ref[pl.ds(c, 1), :] = arrived[recv_ref[first + c]]
        out_ref[pl.ds(first, chunk), :] = stage_ref[...].astype(jnp.bfloat16)

    @pl.loop(1, count)
    def _(j):
        copy_to(j).wait_send()


def relay(blended, send_slot, recv_slot, axis):
    rows, channels = blended.shape
    count = lax.axis_size(axis)
    capacity = send_slot.shape[0] // count
    chunk = 128
    whole = pl.BlockSpec(memory_space=pltpu.VMEM)
    scalars = pl.BlockSpec(memory_space=pltpu.SMEM)
    boxes = pltpu.VMEM((count, capacity, channels), jnp.bfloat16)
    return pl.pallas_call(
        functools.partial(relay_kernel, axis=axis, count=count),
        out_shape=jax.ShapeDtypeStruct((rows, channels), jnp.bfloat16),
        in_specs=[scalars, scalars, whole],
        out_specs=whole,
        scratch_shapes=[
            pltpu.VMEM((rows + 8, channels), jnp.float32),
            pltpu.VMEM((chunk, channels), jnp.float32),
            boxes,
            boxes,
            pltpu.VMEM((count * capacity, channels), jnp.float32),
            pltpu.SemaphoreType.DMA((count,)),
            pltpu.SemaphoreType.DMA((count,)),
        ],
        compiler_params=pltpu.CompilerParams(
            collective_id=0, has_side_effects=True, vmem_limit_bytes=48 * 1024 * 1024
        ),
    )(send_slot, recv_slot, blended)


def spread_weights(mine):
    slabs, groups = lax.axis_size("brick"), lax.axis_size("grp")
    core = lax.rem(lax.axis_index("brick"), 2)
    part = mine.shape[1] // 2
    half = lax.dynamic_slice_in_dim(mine, core * part, part, axis=1)
    got = [
        lax.ppermute(half, "grp", [(i, (i + j) % groups) for i in range(groups)])
        for j in range(1, groups)
    ]
    got = jnp.stack(got)
    passed = lax.ppermute(got, "brick", [(i, i ^ 1) for i in range(slabs)])
    place = jnp.stack([lax.axis_index("grp"), core]).astype(jnp.int32)
    return place, mine, got, passed


def body(
    features, neighbors, send_low, send_high, send_slot, recv_slot, kernel, norm_gain, norm_shift
):
    row_count, channels = features.shape
    weights = spread_weights(kernel.transpose(0, 2, 1))
    upward, downward = pick_halo(features, send_high, send_low)
    from_lower = shifted(upward, "brick", 1)
    from_upper = shifted(downward, "brick", -1)
    lists, places = compact(neighbors.T, row_count + 2 * send_low.shape[0])
    blended = conv_block(
        features,
        from_lower,
        from_upper,
        lists,
        places,
        weights,
        jnp.broadcast_to(norm_gain[:, None], (channels, BLOCK)),
        jnp.broadcast_to(norm_shift[:, None], (channels, BLOCK)),
    )
    return relay(blended, send_slot, recv_slot, "brick")


def solution(mesh):
    return jax.shard_map(
        body,
        mesh=mesh,
        in_specs=(
            P(("brick", "grp"), None),
            P(("brick", "grp"), None),
            P(("brick", "grp")),
            P(("brick", "grp")),
            P(("brick", "grp")),
            P(("brick", "grp")),
            P(None, None, "grp"),
            P(),
            P(),
        ),
        out_specs=P(("brick", "grp"), None),
        check_vma=False,
    )
```

```python
import functools

import jax
import jax.numpy as jnp
from jax import lax
from jax.experimental import pallas as pl
from jax.experimental.pallas import tpu as pltpu
from jax.sharding import PartitionSpec as P

BLOCK = 256


def shifted(block, axis, distance):
    devices = range(lax.axis_size(axis))
    route = [(i - distance, i) for i in devices if i - distance in devices]
    return lax.ppermute(block, axis, route)


def pick_kernel(high_ref, low_ref, feat_ref, upward_ref, downward_ref, table_ref, stage_ref):
    rows, channels = feat_ref.shape
    chunk = stage_ref.shape[0]
    table = table_ref.reshape(rows, 1, channels)

    @pl.loop(0, rows // chunk)
    def _(i):
        at = pl.ds(pl.multiple_of(i * chunk, chunk), chunk)
        table_ref[at, :] = feat_ref[at, :].astype(jnp.float32)

    for index_ref, into_ref in ((high_ref, upward_ref), (low_ref, downward_ref)):

        @pl.loop(0, into_ref.shape[0] // chunk)
        def _(i, index_ref=index_ref, into_ref=into_ref):
            first = pl.multiple_of(i * chunk, chunk)
            for c in range(chunk):
                stage_ref[pl.ds(c, 1), :] = table[index_ref[first + c]]
            into_ref[pl.ds(first, chunk), :] = stage_ref[...].astype(jnp.bfloat16)


def pick_halo(features, send_high, send_low):
    rows, channels = features.shape
    halo = send_high.shape[0]
    chunk = 256
    whole = pl.BlockSpec(memory_space=pltpu.VMEM)
    scalars = pl.BlockSpec(memory_space=pltpu.SMEM)
    shape = jax.ShapeDtypeStruct((halo, channels), jnp.bfloat16)
    return pl.pallas_call(
        pick_kernel,
        out_shape=(shape, shape),
        in_specs=[scalars, scalars, whole],
        out_specs=(whole, whole),
        scratch_shapes=[
            pltpu.VMEM((rows, channels), jnp.float32),
            pltpu.VMEM((chunk, channels), jnp.float32),
        ],
        compiler_params=pltpu.CompilerParams(vmem_limit_bytes=16 * 1024 * 1024),
    )(send_high, send_low, features)


def compact_kernel(nb_ref, list_ref, pos_ref, *, absent, block):
    offsets, width = nb_ref.shape
    value = nb_ref[...]
    present = value != absent
    lane = lax.broadcasted_iota(jnp.int32, (offsets, width), 1) & (block - 1)
    before = lax.broadcasted_iota(jnp.int32, (block, block), 0)
    after = lax.broadcasted_iota(jnp.int32, (block, block), 1)
    triangle = jnp.where(before <= after, 1.0, 0.0).astype(jnp.bfloat16)
    ones = jnp.where(present, 1.0, 0.0).astype(jnp.bfloat16)
    counted = [
        jnp.dot(ones[:, at : at + block], triangle, preferred_element_type=jnp.float32)
        for at in range(0, width, block)
    ]
    pos = jnp.concatenate(counted, axis=1).astype(jnp.int32) - 1
    pos_ref[...] = jnp.where(present, pos, -1)
    word = jnp.where(present, value + (lane - pos) * 16384 + (1 << 23), 0)
    for bit in range(block.bit_length() - 1):
        moves = (word & (16384 << bit)) != 0
        moved = pltpu.roll(jnp.where(moves, word, 0), width - (1 << bit), 1)
        word = jnp.where(moves, 0, word) + moved
    listed = jnp.where(word != 0, word & 16383, absent)
    half = list_ref.shape[2]
    stride = list_ref.shape[1] // 2
    for i in range(list_ref.shape[0]):
        for h in range(2):
            at = i * block + h * half
            list_ref[i, h * stride : h * stride + offsets, :] = listed[:, at : at + half]


def conv_kernel(
    list_ref,
    next_ref,
    pos_ref,
    feat_ref,
    low_ref,
    up_ref,
    place_ref,
    mine_ref,
    got_ref,
    passed_ref,
    gain_ref,
    shift_ref,
    out_ref,
    w_ref,
    tab_ref,
    buf_a,
    buf_b,
    buf_c,
    acc_ref,
    done_ref,
):
    step = pl.program_id(0)
    steps = pl.num_programs(0) - 1
    rows, channels = feat_ref.shape
    halo = low_ref.shape[0]
    offsets, block = pos_ref.shape
    half = block // 2
    second = list_ref.shape[0] // 2
    middle = offsets // 2
    absent = rows + 2 * halo
    table = tab_ref.reshape(tab_ref.shape[0], 1, channels)
    slots = lax.broadcasted_iota(jnp.int32, (half, block), 0)
    slots = slots.astype(jnp.float32).astype(jnp.bfloat16)
    one, zero = jnp.bfloat16(1), jnp.bfloat16(0)

    @pl.when(step == 0)
    def _():
        chunk = 256
        for src, start in ((feat_ref, 0), (low_ref, rows), (up_ref, rows + halo)):

            @pl.loop(0, src.shape[0] // chunk)
            def _(i, src=src, start=start):
                at = pl.multiple_of(i * chunk, chunk)
                tab_ref[pl.ds(start + at, chunk), :] = src[pl.ds(at, chunk), :].astype(jnp.float32)

        tab_ref[pl.ds(absent, 8), :] = jnp.zeros((8, channels), jnp.float32)

        columns = mine_ref.shape[1]
        part = columns // 2
        groups = got_ref.shape[0] + 1
        group, core = place_ref[0], place_ref[1]
        at = pl.multiple_of(group * columns, columns)
        w_ref[:, pl.ds(at, columns), :] = mine_ref[...]
        for j in range(groups - 1):
            source = lax.rem(group - j - 1 + groups, groups)
            for ref, which in ((got_ref, core), (passed_ref, 1 - core)):
                at = pl.multiple_of(source * columns + which * part, part)
                w_ref[:, pl.ds(at, part), :] = ref[j]

    def offset_of(pair, j):
        at = 2 * pair + j
        return at + jnp.where(at >= middle, 1, 0)

    def gather(pair, buf, base=0, count=2, lists=list_ref):
        for j in range(2 * count):
            k = offset_of(pair, j)
            first = k * half + (second if base else 0)
            for c in range(half):
                buf[pl.ds(j * half + c, 1), :] = table[lists[first + c]]

    def multiply(pair, buf, base=0, count=2):
        products, spreads = [], []
        for j in range(2 * count):
            k = offset_of(pair, j)
            rows_in = buf[j * half : (j + 1) * half, :].astype(jnp.bfloat16)
            products.append(
                lax.dot_general(
                    w_ref[k], rows_in, (((1,), (1,)), ((), ())), preferred_element_type=jnp.float32
                )
            )
            wanted = (pos_ref[pl.ds(k, 1), :] - base).astype(jnp.float32).astype(jnp.bfloat16)
            spreads.append(jnp.where(slots == wanted, one, zero))
        product = jnp.concatenate(products, axis=1)
        high = product.astype(jnp.bfloat16)
        low = (product - high.astype(jnp.float32)).astype(jnp.bfloat16)
        both = jnp.concatenate([high, low], axis=0)
        spread = jnp.concatenate(spreads, axis=0)
        result = jnp.dot(both, spread, preferred_element_type=jnp.float32)
        acc_ref[...] += result[:channels] + result[channels:]

    def own_rows(at):
        return feat_ref[pl.ds(pl.multiple_of(at * block, block), block), :]

    def finish(at):
        summed = done_ref[...]
        centered = summed - jnp.mean(summed, axis=0, keepdims=True)
        spread_sq = jnp.mean(centered * centered, axis=0, keepdims=True)
        normed = centered * lax.rsqrt(spread_sq + 1e-05) * gain_ref[...] + shift_ref[...]
        active = normed / (1.0 + jnp.exp(-normed))
        blended = own_rows(at).astype(jnp.float32) + active.T
        out_ref[...] = blended.astype(jnp.bfloat16)

    pairs = middle

    @pl.when(step == 0)
    def _():
        gather(0, buf_a)

    @pl.when(step < steps)
    def _():
        gather(2, buf_b)
        finish(jnp.maximum(step - 1, 0))
        acc_ref[...] = lax.dot_general(
            w_ref[middle],
            own_rows(step),
            (((1,), (1,)), ((), ())),
            preferred_element_type=jnp.float32,
        )
        multiply(0, buf_a)

        @pl.loop(0, (pairs - 5) // 4)
        def _(p):
            first = 4 * p + 2
            gather(first + 2, buf_a)
            multiply(first, buf_b)
            gather(first + 4, buf_b)
            multiply(first + 2, buf_a)

        gather(pairs - 1, buf_c, count=1)
        multiply(pairs - 3, buf_b)

        crowded = jnp.int32(0)
        for k in range(offsets):
            if k != middle:
                crowded = crowded + jnp.where(list_ref[second + k * half] != absent, 1, 0)

        @pl.when(crowded > 0)
        def _():

            @pl.loop(0, pairs)
            def _(p):
                more = (list_ref[second + offset_of(p, 0) * half] != absent) | (
                    list_ref[second + offset_of(p, 1) * half] != absent
                )

                @pl.when(more)
                def _():
                    gather(p, buf_b, half, 1)
                    multiply(p, buf_b, half, 1)

        gather(0, buf_a, lists=next_ref)
        multiply(pairs - 1, buf_c, count=1)
        done_ref[...] = acc_ref[...]

    @pl.when(step == steps)
    def _():
        finish(steps - 1)


def compact(columns, absent):
    offsets, rows = columns.shape
    width = 8 * BLOCK
    stride = -(-offsets // 8) * 8
    lists = (width // BLOCK, 2 * stride, BLOCK // 2)
    spec = pl.BlockSpec((offsets, width), lambda i: (0, i))
    listed, places = pl.pallas_call(
        functools.partial(compact_kernel, absent=absent, block=BLOCK),
        grid=(rows // width,),
        out_shape=(
            jax.ShapeDtypeStruct((rows // BLOCK, *lists[1:]), jnp.int32),
            jax.ShapeDtypeStruct((offsets, rows), jnp.int32),
        ),
        in_specs=[spec],
        out_specs=(pl.BlockSpec(lists, lambda i: (i, 0, 0)), spec),
        cost_estimate=pl.CostEstimate(
            flops=0, bytes_accessed=200 * rows * offsets, transcendentals=0
        ),
    )(columns)
    return listed.reshape(-1), places


def conv_block(features, from_lower, from_upper, lists, places, weights, gain, shift):
    place, mine, got, passed = weights
    rows, channels = features.shape
    halo = from_lower.shape[0]
    offsets = places.shape[0]
    block = BLOCK
    span = lists.shape[0] // (rows // block)
    whole = pl.BlockSpec(memory_space=pltpu.VMEM)
    last = rows // block - 1
    return pl.pallas_call(
        conv_kernel,
        grid=(rows // block + 1,),
        out_shape=jax.ShapeDtypeStruct((rows, channels), jnp.bfloat16),
        in_specs=[
            pl.BlockSpec((span,), lambda i: (jnp.minimum(i, last),), memory_space=pltpu.SMEM),
            pl.BlockSpec((span,), lambda i: (jnp.minimum(i + 1, last),), memory_space=pltpu.SMEM),
            pl.BlockSpec((offsets, block), lambda i: (0, jnp.minimum(i, last))),
            whole,
            whole,
            whole,
            pl.BlockSpec(memory_space=pltpu.SMEM),
            whole,
            whole,
            whole,
            whole,
            whole,
        ],
        out_specs=pl.BlockSpec((block, channels), lambda i: (jnp.maximum(i - 1, 0), 0)),
        scratch_shapes=[
            pltpu.VMEM((offsets, channels, channels), jnp.bfloat16),
            pltpu.VMEM((rows + 2 * halo + 8, channels), jnp.float32),
            pltpu.VMEM((2 * block, channels), jnp.float32),
            pltpu.VMEM((2 * block, channels), jnp.float32),
            pltpu.VMEM((block, channels), jnp.float32),
            pltpu.VMEM((channels, block), jnp.float32),
            pltpu.VMEM((channels, block), jnp.float32),
        ],
        compiler_params=pltpu.CompilerParams(vmem_limit_bytes=48 * 1024 * 1024),
        cost_estimate=pl.CostEstimate(
            flops=2 * rows * offsets * channels * channels,
            bytes_accessed=8 * rows * channels,
            transcendentals=rows * channels,
        ),
    )(
        lists,
        lists,
        places,
        features,
        from_lower,
        from_upper,
        place,
        mine,
        got,
        passed,
        gain,
        shift,
    )


def relay_kernel(
    send_ref,
    recv_ref,
    rows_ref,
    out_ref,
    table_ref,
    stage_ref,
    outbox_ref,
    inbox_ref,
    arrived_ref,
    send_sem,
    recv_sem,
    *,
    axis,
    count,
):
    me = lax.axis_index(axis)
    rows, channels = rows_ref.shape
    capacity = outbox_ref.shape[1]
    chunk = stage_ref.shape[0]
    table = table_ref.reshape(table_ref.shape[0], 1, channels)
    arrived = arrived_ref.reshape(arrived_ref.shape[0], 1, channels)

    barrier = pltpu.get_barrier_semaphore()

    @pl.loop(1, count)
    def _(j):
        pl.semaphore_signal(
            barrier,
            inc=1,
            device_id={axis: lax.rem(me + j, count)},
            device_id_type=pl.DeviceIdType.MESH,
        )

    @pl.loop(0, rows // chunk)
    def _(i):
        at = pl.ds(pl.multiple_of(i * chunk, chunk), chunk)
        table_ref[at, :] = rows_ref[at, :].astype(jnp.float32)

    table_ref[pl.ds(rows, 8), :] = jnp.zeros((8, channels), jnp.float32)
    pl.semaphore_wait(barrier, count - 1)

    def copy_to(j):
        to = lax.rem(me + j, count)
        return pltpu.make_async_remote_copy(
            src_ref=outbox_ref.at[to],
            dst_ref=inbox_ref.at[me],
            send_sem=send_sem.at[j],
            recv_sem=recv_sem.at[j],
            device_id={axis: to},
            device_id_type=pl.DeviceIdType.MESH,
        )

    def fill(shard, into_ref):
        @pl.loop(0, capacity // chunk)
        def _(i):
            first = pl.multiple_of(i * chunk, chunk)
            for c in range(chunk):
                stage_ref[pl.ds(c, 1), :] = table[send_ref[shard * capacity + first + c]]
            into_ref[pl.ds(first, chunk), :] = stage_ref[...].astype(jnp.bfloat16)

    @pl.loop(0, count - 1)
    def _(i):
        j = lax.rem(i + count // 2, count - 1) + 1
        fill(lax.rem(me + j, count), outbox_ref.at[lax.rem(me + j, count)])
        copy_to(j).start()

    fill(me, inbox_ref.at[me])

    def widen(source):
        @pl.loop(0, capacity // chunk)
        def _(i):
            first = pl.multiple_of(i * chunk, chunk)
            to = pl.multiple_of(source * capacity + first, chunk)
            arrived_ref[pl.ds(to, chunk), :] = inbox_ref[source, pl.ds(first, chunk), :].astype(
                jnp.float32
            )

    widen(me)

    @pl.loop(0, count - 1)
    def _(i):
        j = lax.rem(i + count // 2, count - 1) + 1
        source = lax.rem(me - j + count, count)
        pltpu.make_async_remote_copy(
            src_ref=outbox_ref.at[source],
            dst_ref=inbox_ref.at[source],
            send_sem=send_sem.at[j],
            recv_sem=recv_sem.at[j],
            device_id={axis: source},
            device_id_type=pl.DeviceIdType.MESH,
        ).wait_recv()
        widen(source)

    @pl.loop(0, rows // chunk)
    def _(i):
        first = pl.multiple_of(i * chunk, chunk)
        for c in range(chunk):
            stage_ref[pl.ds(c, 1), :] = arrived[recv_ref[first + c]]
        out_ref[pl.ds(first, chunk), :] = stage_ref[...].astype(jnp.bfloat16)

    @pl.loop(1, count)
    def _(j):
        copy_to(j).wait_send()


def relay(blended, send_slot, recv_slot, axis):
    rows, channels = blended.shape
    count = lax.axis_size(axis)
    capacity = send_slot.shape[0] // count
    chunk = 128
    whole = pl.BlockSpec(memory_space=pltpu.VMEM)
    scalars = pl.BlockSpec(memory_space=pltpu.SMEM)
    boxes = pltpu.VMEM((count, capacity, channels), jnp.bfloat16)
    return pl.pallas_call(
        functools.partial(relay_kernel, axis=axis, count=count),
        out_shape=jax.ShapeDtypeStruct((rows, channels), jnp.bfloat16),
        in_specs=[scalars, scalars, whole],
        out_specs=whole,
        scratch_shapes=[
            pltpu.VMEM((rows + 8, channels), jnp.float32),
            pltpu.VMEM((chunk, channels), jnp.float32),
            boxes,
            boxes,
            pltpu.VMEM((count * capacity, channels), jnp.float32),
            pltpu.SemaphoreType.DMA((count,)),
            pltpu.SemaphoreType.DMA((count,)),
        ],
        compiler_params=pltpu.CompilerParams(
            collective_id=0, has_side_effects=True, vmem_limit_bytes=48 * 1024 * 1024
        ),
    )(send_slot, recv_slot, blended)


def spread_weights(mine):
    slabs, groups = lax.axis_size("brick"), lax.axis_size("grp")
    core = lax.rem(lax.axis_index("brick"), 2)
    part = mine.shape[1] // 2
    half = lax.dynamic_slice_in_dim(mine, core * part, part, axis=1)
    got = [
        lax.ppermute(half, "grp", [(i, (i + j) % groups) for i in range(groups)])
        for j in range(1, groups)
    ]
    got = jnp.stack(got)
    passed = lax.ppermute(got, "brick", [(i, i ^ 1) for i in range(slabs)])
    place = jnp.stack([lax.axis_index("grp"), core]).astype(jnp.int32)
    return place, mine, got, passed


def body(
    features, neighbors, send_low, send_high, send_slot, recv_slot, kernel, norm_gain, norm_shift
):
    row_count, channels = features.shape
    weights = spread_weights(kernel.transpose(0, 2, 1))
    upward, downward = pick_halo(features, send_high, send_low)
    from_lower = shifted(upward, "brick", 1)
    from_upper = shifted(downward, "brick", -1)
    lists, places = compact(neighbors.T, row_count + 2 * send_low.shape[0])
    blended = conv_block(
        features,
        from_lower,
        from_upper,
        lists,
        places,
        weights,
        jnp.broadcast_to(norm_gain[:, None], (channels, BLOCK)),
        jnp.broadcast_to(norm_shift[:, None], (channels, BLOCK)),
    )
    return relay(blended, send_slot, recv_slot, "brick")


def solution(mesh):
    return jax.shard_map(
        body,
        mesh=mesh,
        in_specs=(
            P(("brick", "grp"), None),
            P(("brick", "grp"), None),
            P(("brick", "grp")),
            P(("brick", "grp")),
            P(("brick", "grp")),
            P(("brick", "grp")),
            P(None, None, "grp"),
            P(),
            P(),
        ),
        out_specs=P(("brick", "grp"), None),
        check_vma=False,
    )
```

```python
import functools

import jax
import jax.numpy as jnp
from jax import lax
from jax.experimental import pallas as pl
from jax.experimental.pallas import tpu as pltpu
from jax.sharding import PartitionSpec as P

BLOCK = 256


def shifted(block, axis, distance):
    devices = range(lax.axis_size(axis))
    route = [(i - distance, i) for i in devices if i - distance in devices]
    return lax.ppermute(block, axis, route)


def pick_kernel(high_ref, low_ref, feat_ref, upward_ref, downward_ref, table_ref, stage_ref):
    rows, channels = feat_ref.shape
    chunk = stage_ref.shape[0]
    table = table_ref.reshape(rows, 1, channels)

    @pl.loop(0, rows // chunk)
    def _(i):
        at = pl.ds(pl.multiple_of(i * chunk, chunk), chunk)
        table_ref[at, :] = feat_ref[at, :].astype(jnp.float32)

    for index_ref, into_ref in ((high_ref, upward_ref), (low_ref, downward_ref)):

        @pl.loop(0, into_ref.shape[0] // chunk)
        def _(i, index_ref=index_ref, into_ref=into_ref):
            first = pl.multiple_of(i * chunk, chunk)
            for c in range(chunk):
                stage_ref[pl.ds(c, 1), :] = table[index_ref[first + c]]
            into_ref[pl.ds(first, chunk), :] = stage_ref[...].astype(jnp.bfloat16)


def pick_halo(features, send_high, send_low):
    rows, channels = features.shape
    halo = send_high.shape[0]
    chunk = 256
    whole = pl.BlockSpec(memory_space=pltpu.VMEM)
    scalars = pl.BlockSpec(memory_space=pltpu.SMEM)
    shape = jax.ShapeDtypeStruct((halo, channels), jnp.bfloat16)
    return pl.pallas_call(
        pick_kernel,
        out_shape=(shape, shape),
        in_specs=[scalars, scalars, whole],
        out_specs=(whole, whole),
        scratch_shapes=[
            pltpu.VMEM((rows, channels), jnp.float32),
            pltpu.VMEM((chunk, channels), jnp.float32),
        ],
        compiler_params=pltpu.CompilerParams(vmem_limit_bytes=16 * 1024 * 1024),
    )(send_high, send_low, features)


def compact_kernel(nb_ref, list_ref, pos_ref, *, absent, block):
    offsets, width = nb_ref.shape
    value = nb_ref[...]
    present = value != absent
    lane = lax.broadcasted_iota(jnp.int32, (offsets, width), 1) & (block - 1)
    before = lax.broadcasted_iota(jnp.int32, (block, block), 0)
    after = lax.broadcasted_iota(jnp.int32, (block, block), 1)
    triangle = jnp.where(before <= after, 1.0, 0.0).astype(jnp.bfloat16)
    ones = jnp.where(present, 1.0, 0.0).astype(jnp.bfloat16)
    counted = [
        jnp.dot(ones[:, at : at + block], triangle, preferred_element_type=jnp.float32)
        for at in range(0, width, block)
    ]
    pos = jnp.concatenate(counted, axis=1).astype(jnp.int32) - 1
    pos_ref[...] = jnp.where(present, pos, -1)
    word = jnp.where(present, value + (lane - pos) * 16384 + (1 << 23), 0)
    for bit in range(block.bit_length() - 1):
        moves = (word & (16384 << bit)) != 0
        moved = pltpu.roll(jnp.where(moves, word, 0), width - (1 << bit), 1)
        word = jnp.where(moves, 0, word) + moved
    listed = jnp.where(word != 0, word & 16383, absent)
    half = list_ref.shape[2]
    stride = list_ref.shape[1] // 2
    for i in range(list_ref.shape[0]):
        for h in range(2):
            at = i * block + h * half
            list_ref[i, h * stride : h * stride + offsets, :] = listed[:, at : at + half]


def conv_kernel(
    list_ref,
    next_ref,
    pos_ref,
    feat_ref,
    low_ref,
    up_ref,
    place_ref,
    mine_ref,
    got_ref,
    passed_ref,
    gain_ref,
    shift_ref,
    out_ref,
    w_ref,
    tab_ref,
    buf_a,
    buf_b,
    acc_ref,
):
    step = pl.program_id(0)
    rows, channels = feat_ref.shape
    halo = low_ref.shape[0]
    offsets, block = pos_ref.shape
    half = block // 2
    second = list_ref.shape[0] // 2
    middle = offsets // 2
    absent = rows + 2 * halo
    table = tab_ref.reshape(tab_ref.shape[0], 1, channels)
    slots = lax.broadcasted_iota(jnp.int32, (half, block), 0)
    slots = slots.astype(jnp.float32).astype(jnp.bfloat16)
    one, zero = jnp.bfloat16(1), jnp.bfloat16(0)

    @pl.when(step == 0)
    def _():
        chunk = 256
        for src, start in ((feat_ref, 0), (low_ref, rows), (up_ref, rows + halo)):

            @pl.loop(0, src.shape[0] // chunk)
            def _(i, src=src, start=start):
                at = pl.multiple_of(i * chunk, chunk)
                tab_ref[pl.ds(start + at, chunk), :] = src[pl.ds(at, chunk), :].astype(jnp.float32)

        tab_ref[pl.ds(absent, 8), :] = jnp.zeros((8, channels), jnp.float32)

        columns = mine_ref.shape[1]
        part = columns // 2
        groups = got_ref.shape[0] + 1
        group, core = place_ref[0], place_ref[1]
        at = pl.multiple_of(group * columns, columns)
        w_ref[:, pl.ds(at, columns), :] = mine_ref[...]
        for j in range(groups - 1):
            source = lax.rem(group - j - 1 + groups, groups)
            for ref, which in ((got_ref, core), (passed_ref, 1 - core)):
                at = pl.multiple_of(source * columns + which * part, part)
                w_ref[:, pl.ds(at, part), :] = ref[j]

    def offset_of(pair, j):
        at = 2 * pair + j
        return at + jnp.where(at >= middle, 1, 0)

    def gather(pair, buf, base=0, count=2, lists=list_ref):
        for j in range(2 * count):
            k = offset_of(pair, j)
            first = k * half + (second if base else 0)
            for c in range(half):
                buf[pl.ds(j * half + c, 1), :] = table[lists[first + c]]

    def multiply(pair, buf, base=0, count=2):
        products, spreads = [], []
        for j in range(2 * count):
            k = offset_of(pair, j)
            rows_in = buf[j * half : (j + 1) * half, :].astype(jnp.bfloat16)
            products.append(
                lax.dot_general(
                    w_ref[k], rows_in, (((1,), (1,)), ((), ())), preferred_element_type=jnp.float32
                )
            )
            wanted = (pos_ref[pl.ds(k, 1), :] - base).astype(jnp.float32).astype(jnp.bfloat16)
            spreads.append(jnp.where(slots == wanted, one, zero))
        product = jnp.concatenate(products, axis=1)
        high = product.astype(jnp.bfloat16)
        low = (product - high.astype(jnp.float32)).astype(jnp.bfloat16)
        both = jnp.concatenate([high, low], axis=0)
        spread = jnp.concatenate(spreads, axis=0)
        result = jnp.dot(both, spread, preferred_element_type=jnp.float32)
        acc_ref[...] += result[:channels] + result[channels:]

    own = feat_ref[pl.ds(pl.multiple_of(step * block, block), block), :]
    pairs = middle

    @pl.when(step == 0)
    def _():
        gather(0, buf_a, count=1)

    acc_ref[...] = lax.dot_general(
        w_ref[middle], own, (((1,), (1,)), ((), ())), preferred_element_type=jnp.float32
    )
    gather(1, buf_b)
    multiply(0, buf_a, count=1)

    @pl.loop(0, (pairs - 3) // 4)
    def _(p):
        first = 1 + 4 * p
        gather(first + 2, buf_a)
        multiply(first, buf_b)
        gather(first + 4, buf_b)
        multiply(first + 2, buf_a)

    gather(pairs - 2, buf_a)
    multiply(pairs - 4, buf_b)

    crowded = jnp.int32(0)
    for k in range(offsets):
        if k != middle:
            crowded = crowded + jnp.where(list_ref[second + k * half] != absent, 1, 0)

    @pl.when(crowded > 0)
    def _():

        @pl.loop(0, pairs)
        def _(p):
            more = (list_ref[second + offset_of(p, 0) * half] != absent) | (
                list_ref[second + offset_of(p, 1) * half] != absent
            )

            @pl.when(more)
            def _():
                gather(p, buf_b, half, 1)
                multiply(p, buf_b, half, 1)

    multiply(pairs - 2, buf_a)
    gather(0, buf_a, count=1, lists=next_ref)
    summed = acc_ref[...].T
    centered = summed - jnp.mean(summed, axis=-1, keepdims=True)
    spread_sq = jnp.mean(centered * centered, axis=-1, keepdims=True)
    normed = centered * lax.rsqrt(spread_sq + 1e-05) * gain_ref[...] + shift_ref[...]
    blended = own.astype(jnp.float32) + normed / (1.0 + jnp.exp(-normed))
    out_ref[...] = blended.astype(jnp.bfloat16)


def compact(columns, absent):
    offsets, rows = columns.shape
    width = 8 * BLOCK
    stride = -(-offsets // 8) * 8
    lists = (width // BLOCK, 2 * stride, BLOCK // 2)
    spec = pl.BlockSpec((offsets, width), lambda i: (0, i))
    listed, places = pl.pallas_call(
        functools.partial(compact_kernel, absent=absent, block=BLOCK),
        grid=(rows // width,),
        out_shape=(
            jax.ShapeDtypeStruct((rows // BLOCK, *lists[1:]), jnp.int32),
            jax.ShapeDtypeStruct((offsets, rows), jnp.int32),
        ),
        in_specs=[spec],
        out_specs=(pl.BlockSpec(lists, lambda i: (i, 0, 0)), spec),
        cost_estimate=pl.CostEstimate(
            flops=0, bytes_accessed=200 * rows * offsets, transcendentals=0
        ),
    )(columns)
    return listed.reshape(-1), places


def conv_block(features, from_lower, from_upper, lists, places, weights, gain, shift):
    place, mine, got, passed = weights
    rows, channels = features.shape
    halo = from_lower.shape[0]
    offsets = places.shape[0]
    block = BLOCK
    span = lists.shape[0] // (rows // block)
    whole = pl.BlockSpec(memory_space=pltpu.VMEM)
    last = rows // block - 1
    return pl.pallas_call(
        conv_kernel,
        grid=(rows // block,),
        out_shape=jax.ShapeDtypeStruct((rows, channels), jnp.bfloat16),
        in_specs=[
            pl.BlockSpec((span,), lambda i: (i,), memory_space=pltpu.SMEM),
            pl.BlockSpec((span,), lambda i: (jnp.minimum(i + 1, last),), memory_space=pltpu.SMEM),
            pl.BlockSpec((offsets, block), lambda i: (0, i)),
            whole,
            whole,
            whole,
            pl.BlockSpec(memory_space=pltpu.SMEM),
            whole,
            whole,
            whole,
            whole,
            whole,
        ],
        out_specs=pl.BlockSpec((block, channels), lambda i: (i, 0)),
        scratch_shapes=[
            pltpu.VMEM((offsets, channels, channels), jnp.bfloat16),
            pltpu.VMEM((rows + 2 * halo + 8, channels), jnp.float32),
            pltpu.VMEM((2 * block, channels), jnp.float32),
            pltpu.VMEM((2 * block, channels), jnp.float32),
            pltpu.VMEM((channels, block), jnp.float32),
        ],
        compiler_params=pltpu.CompilerParams(vmem_limit_bytes=48 * 1024 * 1024),
        cost_estimate=pl.CostEstimate(
            flops=2 * rows * offsets * channels * channels,
            bytes_accessed=8 * rows * channels,
            transcendentals=rows * channels,
        ),
    )(
        lists,
        lists,
        places,
        features,
        from_lower,
        from_upper,
        place,
        mine,
        got,
        passed,
        gain,
        shift,
    )


def relay_kernel(
    send_ref,
    recv_ref,
    rows_ref,
    out_ref,
    table_ref,
    stage_ref,
    outbox_ref,
    inbox_ref,
    arrived_ref,
    send_sem,
    recv_sem,
    *,
    axis,
    count,
):
    me = lax.axis_index(axis)
    rows, channels = rows_ref.shape
    capacity = outbox_ref.shape[1]
    chunk = stage_ref.shape[0]
    table = table_ref.reshape(table_ref.shape[0], 1, channels)
    arrived = arrived_ref.reshape(arrived_ref.shape[0], 1, channels)

    barrier = pltpu.get_barrier_semaphore()

    @pl.loop(1, count)
    def _(j):
        pl.semaphore_signal(
            barrier,
            inc=1,
            device_id={axis: lax.rem(me + j, count)},
            device_id_type=pl.DeviceIdType.MESH,
        )

    @pl.loop(0, rows // chunk)
    def _(i):
        at = pl.ds(pl.multiple_of(i * chunk, chunk), chunk)
        table_ref[at, :] = rows_ref[at, :].astype(jnp.float32)

    table_ref[pl.ds(rows, 8), :] = jnp.zeros((8, channels), jnp.float32)
    pl.semaphore_wait(barrier, count - 1)

    bits = count.bit_length() - 1
    axis_bits = (bits - 1) // 2
    core = lax.rem(me, 2)

    def exchanged(distance):
        if bits != 2 * axis_bits + 1:
            return distance
        span = 1 << axis_bits
        return distance % 2 + 2 * (distance // 2 % span * span + distance // 2 // span)

    plane = sorted(range(2, count, 2), key=lambda d: -(exchanged(d) == d))
    order = plane + [d + 1 for d in plane] + [1]

    def distance_at(i):
        d = jnp.int32(0)
        for at, here in enumerate(order):
            d = jnp.where(i == at, here + core * (exchanged(here) - here), d)
        return d

    def partner(distance):
        at = jnp.int32(0)
        for bit in range(bits):
            scale = 1 << bit
            at = at + scale * lax.rem(me // scale + distance // scale, 2)
        return at

    def copy_to(j):
        to = partner(j)
        return pltpu.make_async_remote_copy(
            src_ref=outbox_ref.at[to],
            dst_ref=inbox_ref.at[me],
            send_sem=send_sem.at[j],
            recv_sem=recv_sem.at[j],
            device_id={axis: to},
            device_id_type=pl.DeviceIdType.MESH,
        )

    def fill(shard, into_ref):
        @pl.loop(0, capacity // chunk)
        def _(i):
            first = pl.multiple_of(i * chunk, chunk)
            for c in range(chunk):
                stage_ref[pl.ds(c, 1), :] = table[send_ref[shard * capacity + first + c]]
            into_ref[pl.ds(first, chunk), :] = stage_ref[...].astype(jnp.bfloat16)

    @pl.loop(0, count - 1)
    def _(i):
        j = distance_at(i)
        to = partner(j)
        fill(to, outbox_ref.at[to])
        copy_to(j).start()

    fill(me, inbox_ref.at[me])

    def widen(source):
        @pl.loop(0, capacity // chunk)
        def _(i):
            first = pl.multiple_of(i * chunk, chunk)
            to = pl.multiple_of(source * capacity + first, chunk)
            arrived_ref[pl.ds(to, chunk), :] = inbox_ref[source, pl.ds(first, chunk), :].astype(
                jnp.float32
            )

    widen(me)

    @pl.loop(0, count - 1)
    def _(i):
        j = distance_at(i)
        source = partner(j)
        pltpu.make_async_remote_copy(
            src_ref=outbox_ref.at[source],
            dst_ref=inbox_ref.at[source],
            send_sem=send_sem.at[j],
            recv_sem=recv_sem.at[j],
            device_id={axis: source},
            device_id_type=pl.DeviceIdType.MESH,
        ).wait_recv()
        widen(source)

    @pl.loop(0, rows // chunk)
    def _(i):
        first = pl.multiple_of(i * chunk, chunk)
        for c in range(chunk):
            stage_ref[pl.ds(c, 1), :] = arrived[recv_ref[first + c]]
        out_ref[pl.ds(first, chunk), :] = stage_ref[...].astype(jnp.bfloat16)

    @pl.loop(1, count)
    def _(j):
        copy_to(j).wait_send()


def relay(blended, send_slot, recv_slot, axis):
    rows, channels = blended.shape
    count = lax.axis_size(axis)
    capacity = send_slot.shape[0] // count
    chunk = 128
    whole = pl.BlockSpec(memory_space=pltpu.VMEM)
    scalars = pl.BlockSpec(memory_space=pltpu.SMEM)
    boxes = pltpu.VMEM((count, capacity, channels), jnp.bfloat16)
    return pl.pallas_call(
        functools.partial(relay_kernel, axis=axis, count=count),
        out_shape=jax.ShapeDtypeStruct((rows, channels), jnp.bfloat16),
        in_specs=[scalars, scalars, whole],
        out_specs=whole,
        scratch_shapes=[
            pltpu.VMEM((rows + 8, channels), jnp.float32),
            pltpu.VMEM((chunk, channels), jnp.float32),
            boxes,
            boxes,
            pltpu.VMEM((count * capacity, channels), jnp.float32),
            pltpu.SemaphoreType.DMA((count,)),
            pltpu.SemaphoreType.DMA((count,)),
        ],
        compiler_params=pltpu.CompilerParams(
            collective_id=0, has_side_effects=True, vmem_limit_bytes=48 * 1024 * 1024
        ),
    )(send_slot, recv_slot, blended)


def spread_weights(mine):
    slabs, groups = lax.axis_size("brick"), lax.axis_size("grp")
    core = lax.rem(lax.axis_index("brick"), 2)
    part = mine.shape[1] // 2
    half = lax.dynamic_slice_in_dim(mine, core * part, part, axis=1)
    got = [
        lax.ppermute(half, "grp", [(i, (i + j) % groups) for i in range(groups)])
        for j in range(1, groups)
    ]
    got = jnp.stack(got)
    passed = lax.ppermute(got, "brick", [(i, i ^ 1) for i in range(slabs)])
    place = jnp.stack([lax.axis_index("grp"), core]).astype(jnp.int32)
    return place, mine, got, passed


def body(
    features, neighbors, send_low, send_high, send_slot, recv_slot, kernel, norm_gain, norm_shift
):
    row_count, channels = features.shape
    weights = spread_weights(kernel.transpose(0, 2, 1))
    upward, downward = pick_halo(features, send_high, send_low)
    from_lower = shifted(upward, "brick", 1)
    from_upper = shifted(downward, "brick", -1)
    lists, places = compact(neighbors.T, row_count + 2 * send_low.shape[0])
    blended = conv_block(
        features,
        from_lower,
        from_upper,
        lists,
        places,
        weights,
        norm_gain.reshape(1, channels),
        norm_shift.reshape(1, channels),
    )
    return relay(blended, send_slot, recv_slot, "brick")


def solution(mesh):
    return jax.shard_map(
        body,
        mesh=mesh,
        in_specs=(
            P(("brick", "grp"), None),
            P(("brick", "grp"), None),
            P(("brick", "grp")),
            P(("brick", "grp")),
            P(("brick", "grp")),
            P(("brick", "grp")),
            P(None, None, "grp"),
            P(),
            P(),
        ),
        out_specs=P(("brick", "grp"), None),
        check_vma=False,
    )
```
